512 devices in a mesh: dp: 16 (over y, core), group: 32 (over x, z).
Axes of the slice: x: 4, y: 8, z: 8, core: 2. Of those that a mesh axis runs over, the one named last changes fastest.
Arguments:
- queries: bfloat16 [65536, 4096], P(('dp', 'group')), may hold values from -6 to 6
- out_grad: bfloat16 [65536, 4096], P(('dp', 'group')), may hold values from -6 to 6
- encodings: bfloat16 [512, 128, 448], P(('dp', 'group')), may hold values from -6 to 6
- key_weight: bfloat16 [448, 4096], P(None, 'group'), may hold values from -0.25 to 0.25
- value_weight: bfloat16 [448, 4096], P(None, 'group'), may hold values from -0.25 to 0.25
- nbr_ids: int32 [1024, 2], P(('dp', 'group')), may hold values from 0 to 511, as said below
Outputs:
- query_grad: bfloat16 [65536, 4096], P(('dp', 'group'))
- enc_grad: bfloat16 [512, 128, 448], P(('dp', 'group'))
- key_weight_grad: float32 [448, 4096], P(None, 'group')
- value_weight_grad: float32 [448, 4096], P(None, 'group')
The draws below stay inside these ranges and needn't reach their ends.
Inputs may be any that keep to these rules, and one draw needn't show every extreme that they name: Each span names two different neighbours, both in its own data group's database: nbr_ids[c, j] // 32 equals c // 64.
All inputs are finite; a program needn't handle non-finite values.
Results may differ from the reference program's by a relative error of at most 0.025.
Values may be sent and summed in bfloat16 or wider, within the bound.
A program may use at most 128 MiB of HBM per device.

```python
import jax
import jax.numpy as jnp
from jax import lax

HEADS = 32
HEAD_DIM = 128
ENC = 448
SPAN = 64
NLEN = 128
HEADS_DEV = 1
SPANS_GROUP = 64
SPANS = 1024
TOKENS = 65536
NB_GROUP = 32
NEIGH = 512
N_DP = 16
N_GROUP = 32


def draw_nbr_ids(key, part):
    key = jax.random.fold_in(key, 7)
    key_one, key_two, key_three = jax.random.split(key, 3)
    first_a = jax.random.randint(key_one, (SPANS,), 0, NB_GROUP, dtype=jnp.int32)
    first_b = jax.random.randint(key_two, (SPANS,), 0, NB_GROUP, dtype=jnp.int32)
    first = jnp.minimum(first_a, first_b)
    first = first.at[0].set(0).at[SPANS - 1].set(0)
    step_on = jax.random.randint(key_three, (SPANS,), 0, NB_GROUP - 1, dtype=jnp.int32)
    second = (first + 1 + step_on) % NB_GROUP
    second = second.at[SPANS - 1].set(NB_GROUP - 1)
    offset = jnp.arange(SPANS, dtype=jnp.int32) // SPANS_GROUP * NB_GROUP
    return jnp.stack([first + offset, second + offset], axis=1).astype(jnp.int32)


def steps_of(own_key, dims, pieces, least, largest):
    loudness, own = 1.0, jax.random.fold_in(own_key, 6)
    for axis_at, parts in pieces:
        heights = jnp.exp(jax.random.uniform(jax.random.fold_in(own, axis_at), (parts,), jnp.float32, least / len(pieces), largest / len(pieces)))
        loudness = loudness * jnp.repeat(heights, dims[axis_at] // parts).reshape([-1 if axis == axis_at else 1 for axis in range(len(dims))])
    return loudness


def bell_draw(key, extent, spread, bound, pieces=(), held_as=jnp.bfloat16):
    values = jax.random.normal(key, extent, jnp.float32) * spread
    if len(pieces) > 0:
        values = steps_of(key, extent, pieces, -0.22, 0.18) * values
    return jnp.clip(values, min=-bound, max=bound).astype(held_as)


def setup_inputs(seed: int = 0) -> dict:
    seeds = jax.random.split(jax.random.key(seed), 7)
    queries = bell_draw(seeds[0], (TOKENS, HEADS * HEAD_DIM), 1.0, 6.0, ((0, 512),))
    out_grad = bell_draw(seeds[1], (TOKENS, HEADS * HEAD_DIM), 1.0, 6.0, ((0, 512),))
    encodings = bell_draw(seeds[2], (NEIGH, NLEN, ENC), 1.0, 6.0, ((0, 512),))
    key_weight = bell_draw(seeds[3], (ENC, HEADS * HEAD_DIM), ENC ** -0.5, 0.25, ((1, 32),))
    value_weight = bell_draw(seeds[4], (ENC, HEADS * HEAD_DIM), ENC ** -0.5, 0.25, ((1, 32),))
    nbr_ids = draw_nbr_ids(jax.random.fold_in(seeds[6], 71), 0)
    return {"queries": queries, "out_grad": out_grad, "encodings": encodings, "key_weight": key_weight, "value_weight": value_weight, "nbr_ids": nbr_ids}


def attend(query_block, grad_block, key_rows, value_rows, slot_ids):
    span_count, span_len, block_width = query_block.shape
    head_count = block_width // HEAD_DIM
    scale = HEAD_DIM ** -0.5
    flat_ids = slot_ids.reshape(-1)
    key_chosen = jnp.take(key_rows, flat_ids, axis=0).reshape(span_count, 2 * NLEN, head_count, HEAD_DIM).astype(jnp.float32)
    value_chosen = jnp.take(value_rows, flat_ids, axis=0).reshape(span_count, 2 * NLEN, head_count, HEAD_DIM).astype(jnp.float32)
    query_four = query_block.reshape(span_count, span_len, head_count, HEAD_DIM).astype(jnp.float32)
    grad_four = grad_block.reshape(span_count, span_len, head_count, HEAD_DIM).astype(jnp.float32)
    scores = jnp.einsum('cqhd,ckhd->chqk', query_four, key_chosen) * scale
    expo = jnp.exp(scores)
    weights = expo / jnp.sum(expo, axis=-1, keepdims=True)
    weights_bf = weights.astype(jnp.bfloat16)
    weight_grad = jnp.einsum('cqhd,ckhd->chqk', grad_four, value_chosen)
    row_delta = jnp.sum(weights * weight_grad, axis=-1, keepdims=True)
    score_grads = (weights * (weight_grad - row_delta) * scale).astype(jnp.bfloat16)
    score_wide = score_grads.astype(jnp.float32)
    query_grads = jnp.einsum('chqk,ckhd->cqhd', score_wide, key_chosen).astype(jnp.bfloat16)
    key_slots = jnp.einsum('chqk,cqhd->ckhd', score_wide, query_four)
    value_slots = jnp.einsum('chqk,cqhd->ckhd', weights_bf.astype(jnp.float32), grad_four)
    return (query_grads.reshape(span_count * span_len, block_width),
            key_slots.reshape(span_count * 2, NLEN, block_width),
            value_slots.reshape(span_count * 2, NLEN, block_width))


def reference(queries, out_grad, encodings, key_weight, value_weight, nbr_ids):
    block_width = HEADS_DEV * HEAD_DIM
    group_rows = SPANS_GROUP * SPAN

    def one_group(group_index):
        enc_rows = lax.dynamic_slice_in_dim(encodings, group_index * NB_GROUP, NB_GROUP, 0)
        enc_wide = enc_rows.astype(jnp.float32)
        query_rows = lax.dynamic_slice_in_dim(queries, group_index * group_rows, group_rows, 0)
        grad_rows = lax.dynamic_slice_in_dim(out_grad, group_index * group_rows, group_rows, 0)
        slot_ids = lax.dynamic_slice_in_dim(nbr_ids, group_index * SPANS_GROUP, SPANS_GROUP, 0) - group_index * NB_GROUP

        def one_block(enc_total, block):
            key_block = lax.dynamic_slice_in_dim(key_weight, block * block_width, block_width, 1).astype(jnp.float32)
            value_block = lax.dynamic_slice_in_dim(value_weight, block * block_width, block_width, 1).astype(jnp.float32)
            key_rows = jnp.einsum('nte,ef->ntf', enc_wide, key_block).astype(jnp.bfloat16)
            value_rows = jnp.einsum('nte,ef->ntf', enc_wide, value_block).astype(jnp.bfloat16)
            query_block = lax.dynamic_slice_in_dim(query_rows, block * block_width, block_width, 1).reshape(SPANS_GROUP, SPAN, block_width)
            grad_block = lax.dynamic_slice_in_dim(grad_rows, block * block_width, block_width, 1).reshape(SPANS_GROUP, SPAN, block_width)
            query_grads, key_slots, value_slots = attend(query_block, grad_block, key_rows, value_rows, slot_ids)
            flat_ids = slot_ids.reshape(-1)
            empty = jnp.zeros((NB_GROUP, NLEN, block_width), jnp.float32)
            key_grads = empty.at[flat_ids].add(key_slots).astype(jnp.bfloat16)
            value_grads = empty.at[flat_ids].add(value_slots).astype(jnp.bfloat16)
            key_wide = key_grads.astype(jnp.float32)
            value_wide = value_grads.astype(jnp.float32)
            enc_part = (jnp.einsum('ntf,ef->nte', key_wide, key_block) + jnp.einsum('ntf,ef->nte', value_wide, value_block)).astype(jnp.bfloat16)
            key_wgrad = jnp.einsum('nte,ntf->ef', enc_wide, key_wide)
            value_wgrad = jnp.einsum('nte,ntf->ef', enc_wide, value_wide)
            return enc_total + enc_part.astype(jnp.float32), (query_grads, key_wgrad, value_wgrad)

        start = jnp.zeros((NB_GROUP, NLEN, ENC), jnp.float32)
        enc_total, stacked = lax.scan(one_block, start, jnp.arange(N_GROUP, dtype=jnp.int32))
        return (enc_total.astype(jnp.bfloat16),) + stacked

    enc_parts, query_parts, key_parts, value_parts = lax.map(one_group, jnp.arange(N_DP, dtype=jnp.int32))
    enc_grad = enc_parts.reshape(NEIGH, NLEN, ENC)
    query_grad = jnp.transpose(query_parts, (0, 2, 1, 3)).reshape(TOKENS, HEADS * HEAD_DIM)
    key_weight_grad = jnp.transpose(jnp.sum(key_parts, axis=0), (1, 0, 2)).reshape(ENC, HEADS * HEAD_DIM)
    value_weight_grad = jnp.transpose(jnp.sum(value_parts, axis=0), (1, 0, 2)).reshape(ENC, HEADS * HEAD_DIM)
    return (query_grad, enc_grad, key_weight_grad, value_weight_grad)
```

```python
import functools

import jax
import jax.numpy as jnp
from jax import lax
from jax.experimental import pallas as pl
from jax.experimental.pallas import tpu as pltpu
from jax.sharding import PartitionSpec as P

HEAD_DIM = 128
SPAN = 64
NLEN = 128
ENC = 448
NX, NZ, NY = 4, 8, 8
HEADS_DEV = 8
WIDTH = HEADS_DEV * HEAD_DIM
SLOTS = 16
TOK = 128
HALF = ENC // 2
MESH = pl.DeviceIdType.MESH
BF16, F32 = jnp.bfloat16, jnp.float32
VMEM_LIMIT = 60 * 1024 * 1024


class Place:
    def __init__(self):
        self.dp, self.group = lax.axis_index("dp"), lax.axis_index("group")
        self.x, self.z = self.group // NZ, self.group % NZ
        self.y, self.core = self.dp // 2, self.dp % 2

    def at_x(self, step):
        return (self.dp, (self.x + step) % NX * NZ + self.z)

    def at_z(self, step):
        return (self.dp, self.x * NZ + (self.z + step) % NZ)

    def at_y(self, step):
        return ((self.y + step) % NY * 2 + self.core, self.group)

    def sibling(self):
        return (self.y * 2 + 1 - self.core, self.group)


def meet(peers):
    barrier = pltpu.get_barrier_semaphore()
    for peer in peers:
        pl.semaphore_signal(barrier, inc=1, device_id=peer, device_id_type=MESH)
    pl.semaphore_wait(barrier, len(peers))


class Copies:
    def __init__(self, send_sems, recv_sems, local_sems):
        self.send_sems, self.recv_sems, self.local_sems = send_sems, recv_sems, local_sems
        self.remote, self.local = [], []

    def push(self, src, dst, peer):
        at = len(self.remote)
        copy = pltpu.make_async_remote_copy(
            src_ref=src,
            dst_ref=dst,
            send_sem=self.send_sems.at[at],
            recv_sem=self.recv_sems.at[at],
            device_id=peer,
            device_id_type=MESH,
        )
        copy.start()
        self.remote.append(copy)
        return copy

    def move(self, src, dst):
        copy = pltpu.make_async_copy(src, dst, self.local_sems.at[len(self.local)])
        copy.start()
        self.local.append(copy)
        return copy


def cols(index, width):
    return pl.ds(pl.multiple_of(index * width, width), width)


IN_PUSHES, IN_MOVES = 64, 6


def bring_in_kernel(
    q_ref, g_ref, enc_ref, kw_ref, vw_ref, ids_ref, qx_ref, gx_ref, enc_all, w_all, ids_all, send_sems, recv_sems, local_sems
):
    me = Place()
    x, z, core = me.x, me.z, me.core
    meet([me.at_x(1), me.at_x(2), me.at_x(3), me.at_z(1), me.at_z(NZ - 1), me.sibling()])
    run = Copies(send_sems, recv_sems, local_sems)
    own_w = [run.move(kw_ref, w_all.at[0, :, cols(z, TOK)]), run.move(vw_ref, w_all.at[1, :, cols(z, TOK)])]
    own_enc = run.move(enc_ref, enc_all.at[x, z])
    run.move(ids_ref, ids_all.at[x])
    from_x = {}
    for step in (1, 3, 2):
        from_x[NX - step] = run.push(enc_ref, enc_all.at[x, z], me.at_x(step))
    late = [run.push(ids_ref, ids_all.at[x], me.at_x(step)) for step in (1, 2, 3)]
    for copy in own_w:
        copy.wait()
    chunks = ["w", 0, 1, 3, 2]
    arrived = {}
    for hop in range(4):
        for chunk in chunks:
            for way in (1, -1):
                block = (z - way * hop + NZ) % NZ
                if hop == 0 and chunk != "w" and way == 1:
                    if chunk == 0:
                        own_enc.wait()
                    else:
                        from_x[chunk].wait_recv()
                if hop > 0:
                    before = arrived[way, hop - 1, chunk]
                    before.wait_recv()
                if chunk == "w":
                    if hop > 0:
                        part = w_all.at[core, :, cols(block, TOK)]
                        late.append(run.push(part, part, me.sibling()))
                    if hop < 3:
                        part = w_all.at[core, :, cols(block, TOK)]
                    else:
                        part = w_all.at[core, pl.ds(0 if way == 1 else HALF, HALF), cols(block, TOK)]
                else:
                    if hop == 3 and (chunk in (0, 1)) != (way == 1):
                        continue
                    part = enc_all.at[(x + chunk) % NX, block]
                arrived[way, hop, chunk] = run.push(part, part, me.at_z(way))
        if hop == 0:
            for src, dst in ((q_ref, qx_ref), (g_ref, gx_ref)):
                for step in (1, 3, 2):
                    peer = me.at_x(step)
                    late.append(run.push(src.at[:, cols((x + step) % NX, WIDTH)], dst.at[x], peer))
                run.move(src.at[:, cols(x, WIDTH)], dst.at[x])
    far = (z + 4) % NZ
    for way in (1, -1):
        arrived[way, 3, "w"].wait_recv()
    part = w_all.at[core, :, cols(far, TOK)]
    late.append(run.push(part, part, me.sibling()))
    for way, chunk in ((1, 0), (1, 1), (-1, 3), (-1, 2)):
        arrived[way, 3, chunk].wait_recv()
    for copy in late:
        copy.wait_recv()
    for copy in run.remote:
        copy.wait_send()
    for copy in run.local[3:]:
        copy.wait()


def bring_in(queries, out_grad, enc_t, key_weight, value_weight, ids):
    whole = pl.BlockSpec(memory_space=pl.ANY)
    return pl.pallas_call(
        bring_in_kernel,
        out_shape=[
            jax.ShapeDtypeStruct((NX, TOK, WIDTH), BF16),
            jax.ShapeDtypeStruct((NX, TOK, WIDTH), BF16),
            jax.ShapeDtypeStruct((NX, NZ, ENC, NLEN), BF16),
            jax.ShapeDtypeStruct((2, ENC, WIDTH), BF16),
            jax.ShapeDtypeStruct((NX, 8, 128), jnp.int32),
        ],
        in_specs=[whole] * 6,
        out_specs=[whole] * 5,
        scratch_shapes=[
            pltpu.SemaphoreType.DMA((IN_PUSHES,)),
            pltpu.SemaphoreType.DMA((IN_PUSHES,)),
            pltpu.SemaphoreType.DMA((IN_MOVES,)),
        ],
        compiler_params=pltpu.CompilerParams(collective_id=0, has_side_effects=True),
    )(queries, out_grad, enc_t, key_weight, value_weight, ids)


def dot(a, b, da=1, db=0):
    return lax.dot_general(a, b, (((da,), (db,)), ((), ())), preferred_element_type=F32)


def attend_kernel(ids_ref, q_ref, g_ref, enc_ref, w_ref, qg_ref, part_ref, wg_ref, enc_sel, w_t, kv_t, slots_t, total):
    scale = HEAD_DIM ** (-0.5)

    def id_of(slot):
        return ids_ref[slot // 4, slot // 2 % 2, slot % 2]

    for slot in range(SLOTS):
        enc_sel[:, slot * NLEN : (slot + 1) * NLEN] = enc_ref[id_of(slot)]
    for kind in range(2):
        for head in range(HEADS_DEV):
            at = kind * WIDTH + head * HEAD_DIM
            w_t[at : at + HEAD_DIM, :] = w_ref[kind, :, head * HEAD_DIM : (head + 1) * HEAD_DIM].T
    total[...] = jnp.zeros_like(total)

    @pl.loop(0, 8)
    def _(span):
        here = cols(span, 2 * NLEN)
        chosen = enc_sel[:, here]
        for tile in range(4):
            rows = pl.ds(tile * 512, 512)
            kv_t[rows, here] = dot(w_t[rows, :], chosen).astype(BF16)

    @pl.loop(0, 8)
    def _(span):
        here = cols(span, 2 * NLEN)
        source, rows = span // 2, cols(span % 2, SPAN)
        for head in range(HEADS_DEV):
            lanes = pl.ds(head * HEAD_DIM, HEAD_DIM)
            query, grad = q_ref[source, rows, lanes], g_ref[source, rows, lanes]
            key_t = kv_t[head * HEAD_DIM : (head + 1) * HEAD_DIM, here]
            value_t = kv_t[WIDTH + head * HEAD_DIM : WIDTH + (head + 1) * HEAD_DIM, here]
            scores = dot(query, key_t)
            weight_grad = dot(grad, value_t)
            expo = jnp.exp((scores - jnp.max(scores, axis=-1, keepdims=True)) * scale)
            weights = expo * (1.0 / jnp.sum(expo, axis=-1, keepdims=True))
            row_delta = jnp.sum(weights * weight_grad, axis=-1, keepdims=True)
            score_grads = (weights * (weight_grad - row_delta) * scale).astype(BF16)
            qg_ref[source, rows, lanes] = dot(score_grads, key_t, 1, 1).astype(BF16)
            slots_t[head * HEAD_DIM : (head + 1) * HEAD_DIM, here] = dot(query, score_grads, 0, 0).astype(BF16)
            slots_t[WIDTH + head * HEAD_DIM : WIDTH + (head + 1) * HEAD_DIM, here] = dot(
                grad, weights.astype(BF16), 0, 0
            ).astype(BF16)

    for kind in range(2):

        @pl.loop(0, 4)
        def _(tile):
            rows = pl.ds(pl.multiple_of(kind * WIDTH + tile * 256, 256), 256)
            wg_ref[kind, :, cols(tile, 256)] = dot(enc_sel[...], slots_t[rows, :], 1, 1).astype(BF16)

    @pl.loop(0, 8)
    def _(span):
        here = cols(span, 2 * NLEN)
        both = dot(w_ref[0], slots_t[0:WIDTH, here]) + dot(w_ref[1], slots_t[WIDTH:, here])
        total[id_of(2 * span)] += both[:, 0:NLEN]
        total[id_of(2 * span + 1)] += both[:, NLEN:]

    @pl.loop(0, NX * NZ)
    def _(block):
        part_ref[block] = total[block].astype(BF16)


def attend(ids, queries, grads, enc_all, w_all):
    vmem = pl.BlockSpec(memory_space=pltpu.VMEM)
    return pl.pallas_call(
        attend_kernel,
        out_shape=[
            jax.ShapeDtypeStruct((NX, TOK, WIDTH), BF16),
            jax.ShapeDtypeStruct((NX * NZ, ENC, NLEN), BF16),
            jax.ShapeDtypeStruct((2, ENC, WIDTH), BF16),
        ],
        in_specs=[pl.BlockSpec(memory_space=pltpu.SMEM)] + [vmem] * 4,
        out_specs=[vmem] * 3,
        scratch_shapes=[
            pltpu.VMEM((ENC, SLOTS * NLEN), BF16),
            pltpu.VMEM((2 * WIDTH, ENC), BF16),
            pltpu.VMEM((2 * WIDTH, SLOTS * NLEN), BF16),
            pltpu.VMEM((2 * WIDTH, SLOTS * NLEN), BF16),
            pltpu.VMEM((NX * NZ, ENC, NLEN), F32),
        ],
        compiler_params=pltpu.CompilerParams(vmem_limit_bytes=VMEM_LIMIT),
    )(ids, queries, grads, enc_all, w_all)


OUT_PUSHES, OUT_MOVES = 64, 1


def send_out_kernel(
    qg_ref, part_ref, wg_ref, out_q, out_enc, out_k, out_v,
    landed, pair, w_sum, x_sum, x_landed, y_sum, y_landed, w_own, w_other, send_sems, recv_sems, local_sems
):
    me = Place()
    x, z, core = me.x, me.z, me.core
    meet(
        [me.at_x(1), me.at_x(2), me.at_x(3), me.at_z(1), me.at_z(NZ - 1), me.sibling()]
        + [me.at_y(step) for step in range(1, NY)]
    )
    run = Copies(send_sems, recv_sems, local_sems)
    late = []
    from_sibling = run.push(wg_ref.at[1 - core], pair, me.sibling())
    arrived = {}
    for chunk, way in ((0, 1), (2, -1), (1, 1), (3, -1)):
        arrived[way, 0, chunk] = run.push(part_ref.at[chunk, (z + 4) % NZ], landed.at[(1 - way) // 2, 0, chunk], me.at_z(way))
    for step in (1, 3, 2):
        late.append(run.push(qg_ref.at[(x + step) % NX], out_q.at[:, cols(x, WIDTH)], me.at_x(step)))
    run.move(qg_ref.at[x], out_q.at[:, cols(x, WIDTH)])
    from_sibling.wait_recv()
    for block in range(NZ):
        here = slice(block * TOK, (block + 1) * TOK)
        w_sum[block] = (wg_ref[core, :, here].astype(F32) + pair[:, here].astype(F32)).astype(BF16)
    for way in (1, -1):
        rows = pl.ds(0 if way == 1 else HALF, HALF)
        arrived[way, 0, 4] = run.push(
            w_sum.at[(z + 4) % NZ, rows], landed.at[(1 - way) // 2, 0, 4, rows], me.at_z(way)
        )
    for hop in range(1, 4):
        for chunk in (4, 0, 2, 1, 3):
            for way in (1, -1):
                lane = (1 - way) // 2
                block = (z + way * (4 - hop) + NZ) % NZ
                slot = landed.at[lane, hop - 1, chunk]
                own = w_sum.at[block] if chunk == 4 else part_ref.at[chunk, block]
                source = slot
                if (way, hop - 1, chunk) in arrived:
                    arrived[way, hop - 1, chunk].wait_recv()
                    if hop == 1 and chunk == 4:
                        mine, rest = (0, HALF) if way == 1 else (HALF, 0)
                        mine, rest = slice(mine, mine + HALF), slice(rest, rest + HALF)
                        slot[mine] = (slot[mine].astype(F32) + own[mine].astype(F32)).astype(BF16)
                        slot[rest] = own[rest]
                    else:
                        slot[...] = (slot[...].astype(F32) + own[...].astype(F32)).astype(BF16)
                else:
                    source = own
                arrived[way, hop, chunk] = run.push(source, landed.at[lane, hop, chunk], me.at_z(way))
    for way in (1, -1):
        arrived[way, 3, 4].wait_recv()
    y_sum[...] = (w_sum[z].astype(F32) + landed[0, 3, 4].astype(F32) + landed[1, 3, 4].astype(F32)).astype(BF16)
    from_y = [run.push(y_sum, y_landed.at[step - 1], me.at_y(step)) for step in range(1, NY)]
    from_x = {}
    for chunk in (0, 2, 1, 3):
        for way in (1, -1):
            arrived[way, 3, chunk].wait_recv()
        x_sum[chunk] = (
            part_ref[chunk, z].astype(F32) + landed[0, 3, chunk].astype(F32) + landed[1, 3, chunk].astype(F32)
        ).astype(BF16)
    for step in (1, 3, 2):
        from_x[step] = run.push(x_sum.at[(x + step) % NX], x_landed.at[step - 1], me.at_x(step))
    whole = y_sum[...].astype(F32)
    for step in range(1, NY):
        from_y[step - 1].wait_recv()
        whole += y_landed[step - 1].astype(F32)
    w_own[...] = whole
    from_sibling = run.push(w_own, w_other, me.sibling())
    enc = x_sum[x].astype(F32)
    for step in (1, 3, 2):
        from_x[step].wait_recv()
        enc += x_landed[step - 1].astype(F32)
    out_enc[...] = enc.astype(BF16)
    from_sibling.wait_recv()

    @pl.when(core == 0)
    def _():
        out_k[...] = w_own[...]
        out_v[...] = w_other[...]

    @pl.when(core == 1)
    def _():
        out_k[...] = w_other[...]
        out_v[...] = w_own[...]

    for copy in late:
        copy.wait_recv()
    for copy in run.remote:
        copy.wait_send()
    for copy in run.local:
        copy.wait()


def send_out(query_grads, part, weight_grads):
    whole, vmem = pl.BlockSpec(memory_space=pl.ANY), pl.BlockSpec(memory_space=pltpu.VMEM)
    block = (ENC, NLEN)
    return pl.pallas_call(
        send_out_kernel,
        out_shape=[
            jax.ShapeDtypeStruct((TOK, NX * WIDTH), BF16),
            jax.ShapeDtypeStruct(block, BF16),
            jax.ShapeDtypeStruct(block, F32),
            jax.ShapeDtypeStruct(block, F32),
        ],
        in_specs=[whole, vmem, vmem],
        out_specs=[whole, vmem, vmem, vmem],
        scratch_shapes=[
            pltpu.VMEM((2, 4, 5) + block, BF16),
            pltpu.VMEM((ENC, WIDTH), BF16),
            pltpu.VMEM((NZ,) + block, BF16),
            pltpu.VMEM((NX,) + block, BF16),
            pltpu.VMEM((NX - 1,) + block, BF16),
            pltpu.VMEM(block, BF16),
            pltpu.VMEM((NY - 1,) + block, BF16),
            pltpu.VMEM(block, F32),
            pltpu.VMEM(block, F32),
            pltpu.SemaphoreType.DMA((OUT_PUSHES,)),
            pltpu.SemaphoreType.DMA((OUT_PUSHES,)),
            pltpu.SemaphoreType.DMA((OUT_MOVES,)),
        ],
        compiler_params=pltpu.CompilerParams(collective_id=1, has_side_effects=True, vmem_limit_bytes=VMEM_LIMIT),
    )(query_grads, part, weight_grads)


def local(queries, out_grad, encodings, key_weight, value_weight, nbr_ids):
    enc_t = jnp.swapaxes(encodings[0], 0, 1)
    ids = jnp.pad(nbr_ids - lax.axis_index("dp") * (NX * NZ), ((0, 6), (0, 126)))
    q_x, g_x, enc_all, w_all, ids_all = bring_in(queries, out_grad, enc_t, key_weight, value_weight, ids)
    query_grads, part, weight_grads = attend(ids_all, q_x, g_x, enc_all.reshape(NX * NZ, ENC, NLEN), w_all)
    query_grad, enc_grad, key_grad, value_grad = send_out(
        query_grads, part.reshape(NX, NZ, ENC, NLEN), weight_grads
    )
    return query_grad, jnp.swapaxes(enc_grad, 0, 1)[None], key_grad, value_grad


def solution(mesh):
    in_specs = (
        P(("dp", "group"), None),
        P(("dp", "group"), None),
        P(("dp", "group"), None, None),
        P(None, "group"),
        P(None, "group"),
        P(("dp", "group"), None),
    )
    out_specs = (
        P(("dp", "group"), None),
        P(("dp", "group"), None, None),
        P(None, "group"),
        P(None, "group"),
    )
    return jax.shard_map(local, mesh=mesh, in_specs=in_specs, out_specs=out_specs, check_vma=False)
```

```python
import functools

import jax
import jax.numpy as jnp
from jax import lax
from jax.experimental import pallas as pl
from jax.experimental.pallas import tpu as pltpu
from jax.sharding import PartitionSpec as P

HEAD_DIM = 128
SPAN = 64
NLEN = 128
ENC = 448
NX, NZ, NY = 4, 8, 8
HEADS_DEV = 8
WIDTH = HEADS_DEV * HEAD_DIM
SLOTS = 16
TOK = 128
IN_A = 336
OUT_A = 256
MESH = pl.DeviceIdType.MESH
BF16, F32 = jnp.bfloat16, jnp.float32
VMEM_LIMIT = 60 * 1024 * 1024


class Place:
    def __init__(self):
        self.dp, self.group = lax.axis_index("dp"), lax.axis_index("group")
        self.x, self.z = self.group // NZ, self.group % NZ
        self.y, self.core = self.dp // 2, self.dp % 2

    def at_x(self, step):
        return (self.dp, (self.x + step) % NX * NZ + self.z)

    def at_z(self, step):
        return (self.dp, self.x * NZ + (self.z + step) % NZ)

    def at_y(self, step):
        return ((self.y + step) % NY * 2 + self.core, self.group)

    def sibling(self):
        return (self.y * 2 + 1 - self.core, self.group)


def meet(peers):
    barrier = pltpu.get_barrier_semaphore()
    for peer in peers:
        pl.semaphore_signal(barrier, inc=1, device_id=peer, device_id_type=MESH)
    pl.semaphore_wait(barrier, len(peers))


class Copies:
    def __init__(self, send_sems, recv_sems, local_sems):
        self.send_sems, self.recv_sems, self.local_sems = send_sems, recv_sems, local_sems
        self.remote, self.local = [], []

    def push(self, src, dst, peer):
        at = len(self.remote)
        copy = pltpu.make_async_remote_copy(
            src_ref=src,
            dst_ref=dst,
            send_sem=self.send_sems.at[at],
            recv_sem=self.recv_sems.at[at],
            device_id=peer,
            device_id_type=MESH,
        )
        copy.start()
        self.remote.append(copy)
        return copy

    def move(self, src, dst):
        copy = pltpu.make_async_copy(src, dst, self.local_sems.at[len(self.local)])
        copy.start()
        self.local.append(copy)
        return copy


def cols(index, width):
    return pl.ds(pl.multiple_of(index * width, width), width)


def dot(a, b, da=1, db=0):
    return lax.dot_general(a, b, (((da,), (db,)), ((), ())), preferred_element_type=F32)


class Gather:
    def __init__(self, run, me, view, rows, cut):
        self.run, self.me, self.view, self.arrived = run, me, view, {}
        self.parts = {1: pl.ds(0, cut), -1: pl.ds(cut, rows - cut)}

    def send(self, hop, way, source=None):
        if hop > 0:
            self.arrived[way, hop - 1].wait_recv()
        block = (self.me.z - way * hop + NZ) % NZ
        there = self.view(block)
        here = there if source is None else source
        if hop == 3:
            here, there = here.at[self.parts[way]], there.at[self.parts[way]]
        self.arrived[way, hop] = self.run.push(here, there, self.me.at_z(way))
        return block

    def end(self):
        for way in (1, -1):
            self.arrived[way, 3].wait_recv()


class Reduce:
    def __init__(self, run, me, own, landed, rows, cut):
        self.run, self.me, self.own, self.landed, self.arrived = run, me, own, landed, {}
        self.parts = {1: pl.ds(0, cut), -1: pl.ds(cut, rows - cut)}

    def send(self, hop, way):
        lane = (1 - way) // 2
        own = self.own((self.me.z + way * (4 - hop) + NZ) % NZ)
        part, rest = self.parts[way], self.parts[-way]
        there = self.landed.at[lane, hop]
        if hop == 0:
            source, there = own.at[part], there.at[part]
        else:
            self.arrived[way, hop - 1].wait_recv()
            source = self.landed.at[lane, hop - 1]
            if hop == 1:
                source[part] = (source[part].astype(F32) + own[part].astype(F32)).astype(BF16)
                source[rest] = own[rest]
            else:
                source[...] = (source[...].astype(F32) + own[...].astype(F32)).astype(BF16)
        self.arrived[way, hop] = self.run.push(source, there, self.me.at_z(way))

    def end(self):
        for way in (1, -1):
            self.arrived[way, 3].wait_recv()
        own = self.own(self.me.z)[...].astype(F32)
        return own + self.landed[0, 3].astype(F32) + self.landed[1, 3].astype(F32)


PUSHES, MOVES = 160, 10


def whole_kernel(
    q_ref, g_ref, enc_ref, kw_ref, vw_ref, ids_ref,
    out_q, ids_all, out_enc, out_w,
    q_x, g_x, enc_all, w_all, ids, enc_sel, w_t, kv_t, slots_t, scores, grads, score_bf, weight_bf, qg,
    slot_grads, part, w_part, w_pair, w_sum, land_a, land_b, land_w, x_b, b_sum, a_sum, x_a, y_sum, y_land, y_own, w_own, w_other,
    send_sems, recv_sems, local_sems
):
    me = Place()
    x, z, core = me.x, me.z, me.core
    scale = HEAD_DIM ** (-0.5)
    meet(
        [me.at_x(1), me.at_x(2), me.at_x(3), me.at_z(1), me.at_z(NZ - 1), me.sibling()]
        + [me.at_y(step) for step in range(1, NY)]
    )
    run = Copies(send_sems, recv_sems, local_sems)
    late = []

    in_a, in_b = pl.ds(0, IN_A), pl.ds(IN_A, ENC - IN_A)
    own_w = [run.move(kw_ref, w_all.at[0, :, cols(z, TOK)]), run.move(vw_ref, w_all.at[1, :, cols(z, TOK)])]
    own_enc = run.move(enc_ref, enc_all.at[x, z])
    run.move(ids_ref, ids_all.at[x]).wait()
    gather_b = Gather(run, me, lambda block: enc_all.at[x, block, in_b], ENC - IN_A, 64)
    for way in (1, -1):
        gather_b.send(0, way, enc_ref.at[in_b])
    from_x = {}
    for step in (1, 3, 2):
        from_x[NX - step] = run.push(enc_ref.at[in_a], enc_all.at[x, z, in_a], me.at_x(step))
    lists = [run.push(ids_ref, ids_all.at[x], me.at_x(step)) for step in (1, 2, 3)]
    for copy in own_w:
        copy.wait()
    gather_w = Gather(run, me, lambda block: w_all.at[core, :, cols(block, TOK)], ENC, ENC // 2)
    for way in (1, -1):
        gather_w.send(0, way)
    inputs_x = {step: [] for step in range(NX)}
    for step in (1, 3, 2):
        for src, dst in ((q_ref, q_x), (g_ref, g_x)):
            copy = run.push(src.at[:, cols((x + step) % NX, WIDTH)], dst.at[x], me.at_x(step))
            inputs_x[NX - step].append(copy)
    own_inputs = [run.move(src.at[:, cols(x, WIDTH)], dst.at[x]) for src, dst in ((q_ref, q_x), (g_ref, g_x))]
    gathers_a = {}
    for chunk in (0, 1, 3, 2):
        gathers_a[chunk] = Gather(
            run, me, lambda block, chunk=chunk: enc_all.at[(x + chunk) % NX, block, in_a], IN_A, 176
        )
    own_enc.wait()
    for hop in range(4):
        for way in (1, -1):
            if hop > 0:
                gather_b.send(hop, way)
                block = gather_w.send(hop, way)
                view = gather_w.view(block)
                late.append(run.push(view, view, me.sibling()))
        for chunk in (0, 1, 3, 2):
            if hop == 0 and chunk != 0:
                from_x[chunk].wait_recv()
            for way in (1, -1):
                gathers_a[chunk].send(hop, way)
    gather_b.end()
    blocks_b = enc_all.at[x, :, in_b]
    from_x_b = [run.push(blocks_b, blocks_b, me.at_x(step)) for step in (1, 3, 2)]
    gather_w.end()
    view = gather_w.view((z + 4) % NZ)
    late.append(run.push(view, view, me.sibling()))
    for copy in late:
        copy.wait_recv()
    for kind in range(2):
        for head in range(HEADS_DEV):
            at = kind * WIDTH + head * HEAD_DIM
            w_t[at : at + HEAD_DIM, :] = w_all[kind, :, head * HEAD_DIM : (head + 1) * HEAD_DIM].T
    slot_grads[SLOTS] = jnp.zeros((ENC, NLEN), F32)
    for copy in lists:
        copy.wait_recv()
    run.move(ids_all, ids).wait()
    for chunk in (0, 1, 3, 2):
        gathers_a[chunk].end()
    for copy in from_x_b:
        copy.wait_recv()

    def id_of(slot):
        return ids[slot // 4, slot // 2 % 2, slot % 2]

    for slot in range(SLOTS):
        neighbour = id_of(slot)
        enc_sel[:, slot * NLEN : (slot + 1) * NLEN] = enc_all[neighbour // NZ, neighbour % NZ]

    @pl.loop(0, 8)
    def _(span):
        here = cols(span, 2 * NLEN)
        chosen = enc_sel[:, here]
        for tile in range(4):
            rows = pl.ds(tile * 512, 512)
            kv_t[rows, here] = dot(w_t[rows, :], chosen).astype(BF16)

    for step in (1, 3, 2, 0):
        source = (x + step) % NX
        if step == 0:
            for copy in own_inputs:
                copy.wait()
        else:
            for copy in inputs_x[step]:
                copy.wait_recv()

        @pl.loop(0, 2)
        def _(turn):
            here, rows = cols(source * 2 + turn, 2 * NLEN), cols(turn, SPAN)
            for head in range(HEADS_DEV):
                lanes, tile = pl.ds(head * HEAD_DIM, HEAD_DIM), pl.ds(head * SPAN, SPAN)
                scores[tile, :] = dot(q_x[source, rows, lanes], kv_t[lanes, here])
                grads[tile, :] = dot(g_x[source, rows, lanes], kv_t[pl.ds(WIDTH + head * HEAD_DIM, HEAD_DIM), here])
            expo = scores[...]
            expo = jnp.exp((expo - jnp.max(expo, axis=-1, keepdims=True)) * scale)
            weights = expo * (1.0 / jnp.sum(expo, axis=-1, keepdims=True))
            weight_bf[...] = weights.astype(BF16)
            weight_grad = grads[...]
            row_delta = jnp.sum(weights * weight_grad, axis=-1, keepdims=True)
            score_bf[...] = (weights * (weight_grad - row_delta) * scale).astype(BF16)
            for head in range(HEADS_DEV):
                lanes, tile = pl.ds(head * HEAD_DIM, HEAD_DIM), pl.ds(head * SPAN, SPAN)
                query, grad = q_x[source, rows, lanes], g_x[source, rows, lanes]
                qg[source, rows, lanes] = dot(score_bf[tile, :], kv_t[lanes, here], 1, 1).astype(BF16)
                slots_t[lanes, here] = dot(query, score_bf[tile, :], 0, 0).astype(BF16)
                slots_t[pl.ds(WIDTH + head * HEAD_DIM, HEAD_DIM), here] = dot(grad, weight_bf[tile, :], 0, 0).astype(BF16)

        if step == 0:
            run.move(qg.at[x], out_q.at[x])
        else:
            late.append(run.push(qg.at[source], out_q.at[x], me.at_x(step)))

    def slot_products(rows):
        @pl.loop(0, 8)
        def _(span):
            here = cols(span, 2 * NLEN)
            both = dot(w_all[0, rows, :], slots_t[0:WIDTH, here]) + dot(w_all[1, rows, :], slots_t[WIDTH:, here])
            slot_grads[2 * span, rows] = both[:, 0:NLEN]
            slot_grads[2 * span + 1, rows] = both[:, NLEN:]

    def neighbour_sum(at_x, at_z, rows):
        neighbour = at_x * NZ + at_z
        total = None
        for span in range(8):
            first, second = id_of(2 * span), id_of(2 * span + 1)
            slot = jnp.where(first == neighbour, 2 * span, jnp.where(second == neighbour, 2 * span + 1, SLOTS))
            term = slot_grads[slot, rows]
            total = term if total is None else total + term
        part[at_x, at_z, rows] = total.astype(BF16)

    out_a, out_b = pl.ds(0, OUT_A), pl.ds(OUT_A, ENC - OUT_A)
    slot_products(out_b)
    from_x = []
    for step in (1, 3, 2, 0):
        at_x = (x + step) % NX

        @pl.loop(0, NZ)
        def _(at_z):
            neighbour_sum(at_x, at_z, out_b)

        if step != 0:
            from_x.append(run.push(part.at[at_x, :, out_b], x_b.at[step - 1], me.at_x(step)))
    slot_products(out_a)
    reduces_a = [
        Reduce(run, me, lambda block, chunk=chunk: part.at[chunk, block, out_a], land_a.at[chunk], OUT_A, OUT_A // 2)
        for chunk in range(NX)
    ]

    @pl.loop(0, NX)
    def _(at_x):
        neighbour_sum(at_x, (z + 4) % NZ, out_a)

    for chunk in range(NX):
        for way in (1, -1):
            reduces_a[chunk].send(0, way)

    @pl.loop(0, NX * (NZ - 1))
    def _(turn):
        neighbour_sum(turn % NX, (z + 5 + turn // NX) % NZ, out_a)

    def weight_products(kind):
        @pl.loop(0, 4)
        def _(tile):
            rows = pl.ds(pl.multiple_of(kind * WIDTH + tile * 256, 256), 256)
            product = dot(enc_sel[...], slots_t[rows, :], 1, 1).astype(BF16)
            w_part[kind, 2 * tile] = product[:, 0:TOK]
            w_part[kind, 2 * tile + 1] = product[:, TOK:]

    weight_products(1 - core)
    from_sibling = run.push(w_part.at[1 - core], w_pair, me.sibling())
    for chunk in range(NX):
        for way in (1, -1):
            reduces_a[chunk].send(1, way)
    weight_products(core)
    from_sibling.wait_recv()

    @pl.loop(0, NZ)
    def _(block):
        w_sum[block] = (w_part[core, block].astype(F32) + w_pair[block].astype(F32)).astype(BF16)

    reduce_w = Reduce(run, me, lambda block: w_sum.at[block], land_w, ENC, ENC // 2)
    reduce_b = Reduce(run, me, lambda block: b_sum.at[block], land_b, ENC - OUT_A, 96)

    def turn_of(reduces, hop):
        for reduce in reduces:
            for way in (1, -1):
                reduce.send(hop, way)

    turn_of([reduce_w], 0)
    turn_of([reduce_w], 1)
    turn_of(reduces_a, 2)
    turn_of([reduce_w], 2)
    turn_of([reduce_w], 3)
    for copy in from_x:
        copy.wait_recv()

    @pl.loop(0, NZ)
    def _(block):
        total = part[x, block, out_b].astype(F32)
        for step in range(NX - 1):
            total += x_b[step, block].astype(F32)
        b_sum[block] = total.astype(BF16)

    turn_of([reduce_b], 0)
    turn_of(reduces_a, 3)
    y_sum[pl.ds(0, ENC)] = reduce_w.end().astype(BF16)
    y_sum[pl.ds(ENC, 64)] = jnp.zeros((64, TOK), BF16)
    y = me.y
    from_y = []
    for step in range(1, NY):
        from_y.append(run.push(y_sum.at[rows_of((y + step) % NY)], y_land.at[step - 1], me.at_y(step)))
    turn_of([reduce_b], 1)
    total = y_sum[rows_of(y)].astype(F32)
    for step in range(1, NY):
        from_y[step - 1].wait_recv()
        total += y_land[step - 1].astype(F32)
    y_own[rows_of(y)] = total.astype(BF16)
    from_y = [run.push(y_own.at[rows_of(y)], y_own.at[rows_of(y)], me.at_y(step)) for step in range(1, NY)]
    turn_of([reduce_b], 2)
    from_x = {}
    for chunk in range(NX):
        a_sum[chunk] = reduces_a[chunk].end().astype(BF16)
    for step in (1, 3, 2):
        from_x[step] = run.push(a_sum.at[(x + step) % NX], x_a.at[step - 1], me.at_x(step))
    turn_of([reduce_b], 3)
    for copy in from_y:
        copy.wait_recv()
    w_own[...] = y_own[pl.ds(0, ENC)].astype(F32)
    from_sibling = run.push(w_own, w_other, me.sibling())
    total = a_sum[x].astype(F32)
    for step in (1, 3, 2):
        from_x[step].wait_recv()
        total += x_a[step - 1].astype(F32)
    out_enc[out_a] = total.astype(BF16)
    out_enc[out_b] = reduce_b.end().astype(BF16)
    from_sibling.wait_recv()

    @pl.when(core == 0)
    def _():
        out_w[0] = w_own[...]
        out_w[1] = w_other[...]

    @pl.when(core == 1)
    def _():
        out_w[0] = w_other[...]
        out_w[1] = w_own[...]

    for copy in late[7:]:
        copy.wait_recv()
    for copy in run.remote:
        copy.wait_send()
    run.local[-1].wait()


def rows_of(index):
    return pl.ds(pl.multiple_of(index * 64, 64), 64)


def whole(queries, out_grad, enc_t, key_weight, value_weight, ids):
    anywhere, vmem = pl.BlockSpec(memory_space=pl.ANY), pl.BlockSpec(memory_space=pltpu.VMEM)
    enc_b = ENC - OUT_A
    bf = lambda *shape: pltpu.VMEM(shape, BF16)
    f32 = lambda *shape: pltpu.VMEM(shape, F32)
    return pl.pallas_call(
        whole_kernel,
        out_shape=[
            jax.ShapeDtypeStruct((NX, TOK, WIDTH), BF16),
            jax.ShapeDtypeStruct((NX, 8, 128), jnp.int32),
            jax.ShapeDtypeStruct((ENC, NLEN), BF16),
            jax.ShapeDtypeStruct((2, ENC, TOK), F32),
        ],
        in_specs=[anywhere] * 6,
        out_specs=[anywhere, anywhere, vmem, vmem],
        scratch_shapes=[
            bf(NX, TOK, WIDTH),
            bf(NX, TOK, WIDTH),
            bf(NX, NZ, ENC, NLEN),
            bf(2, ENC, WIDTH),
            pltpu.SMEM((NX, 8, 128), jnp.int32),
            bf(ENC, SLOTS * NLEN),
            bf(2 * WIDTH, ENC),
            bf(2 * WIDTH, SLOTS * NLEN),
            bf(2 * WIDTH, SLOTS * NLEN),
            f32(HEADS_DEV * SPAN, 2 * NLEN),
            f32(HEADS_DEV * SPAN, 2 * NLEN),
            bf(HEADS_DEV * SPAN, 2 * NLEN),
            bf(HEADS_DEV * SPAN, 2 * NLEN),
            bf(NX, TOK, WIDTH),
            f32(SLOTS + 1, ENC, NLEN),
            bf(NX, NZ, ENC, NLEN),
            bf(2, NZ, ENC, TOK),
            bf(NZ, ENC, TOK),
            bf(NZ, ENC, TOK),
            bf(NX, 2, 4, OUT_A, NLEN),
            bf(2, 4, enc_b, NLEN),
            bf(2, 4, ENC, TOK),
            bf(NX - 1, NZ, enc_b, NLEN),
            bf(NZ, enc_b, NLEN),
            bf(NX, OUT_A, NLEN),
            bf(NX - 1, OUT_A, NLEN),
            bf(512, TOK),
            bf(NY - 1, 64, TOK),
            bf(512, TOK),
            f32(ENC, TOK),
            f32(ENC, TOK),
            pltpu.SemaphoreType.DMA((PUSHES,)),
            pltpu.SemaphoreType.DMA((PUSHES,)),
            pltpu.SemaphoreType.DMA((MOVES,)),
        ],
        compiler_params=pltpu.CompilerParams(collective_id=0, has_side_effects=True, vmem_limit_bytes=VMEM_LIMIT),
    )(queries, out_grad, enc_t, key_weight, value_weight, ids)


def close_kernel(q_ref, enc_ref, w_ref, out_q, out_enc, out_k, out_v, sems):
    copies = [
        pltpu.make_async_copy(q_ref.at[source], out_q.at[:, pl.ds(source * WIDTH, WIDTH)], sems.at[source])
        for source in range(NX)
    ]
    copies.append(pltpu.make_async_copy(enc_ref, out_enc, sems.at[4]))
    copies.append(pltpu.make_async_copy(w_ref.at[0], out_k, sems.at[5]))
    copies.append(pltpu.make_async_copy(w_ref.at[1], out_v, sems.at[6]))
    for copy in copies:
        copy.start()
    for copy in copies:
        copy.wait()


def close(query_grads, enc_grad, weight_grads):
    anywhere, vmem = pl.BlockSpec(memory_space=pl.ANY), pl.BlockSpec(memory_space=pltpu.VMEM)
    return pl.pallas_call(
        close_kernel,
        out_shape=[
            jax.ShapeDtypeStruct((TOK, NX * WIDTH), BF16),
            jax.ShapeDtypeStruct((ENC, NLEN), BF16),
            jax.ShapeDtypeStruct((ENC, TOK), F32),
            jax.ShapeDtypeStruct((ENC, TOK), F32),
        ],
        in_specs=[anywhere] * 3,
        out_specs=[vmem] * 4,
        scratch_shapes=[pltpu.SemaphoreType.DMA((7,))],
        compiler_params=pltpu.CompilerParams(vmem_limit_bytes=VMEM_LIMIT),
    )(query_grads, enc_grad, weight_grads)


def local(queries, out_grad, encodings, key_weight, value_weight, nbr_ids):
    enc_t = jnp.swapaxes(encodings[0], 0, 1)
    ids = jnp.pad(nbr_ids - lax.axis_index("dp") * (NX * NZ), ((0, 6), (0, 126)))
    query_grads, _, enc_grad, weight_grads = whole(queries, out_grad, enc_t, key_weight, value_weight, ids)
    query_grad, enc_grad, key_grad, value_grad = close(query_grads, enc_grad, weight_grads)
    return query_grad, jnp.swapaxes(enc_grad, 0, 1)[None], key_grad, value_grad


def solution(mesh):
    in_specs = (
        P(("dp", "group"), None),
        P(("dp", "group"), None),
        P(("dp", "group"), None, None),
        P(None, "group"),
        P(None, "group"),
        P(("dp", "group"), None),
    )
    out_specs = (
        P(("dp", "group"), None),
        P(("dp", "group"), None, None),
        P(None, "group"),
        P(None, "group"),
    )
    return jax.shard_map(local, mesh=mesh, in_specs=in_specs, out_specs=out_specs, check_vma=False)
```

```python
import functools

import jax
import jax.numpy as jnp
from jax import lax
from jax.experimental import pallas as pl
from jax.experimental.pallas import tpu as pltpu
from jax.sharding import PartitionSpec as P

HEAD_DIM = 128
SPAN = 64
NLEN = 128
ENC = 448
NX, NZ, NY = 4, 8, 8
HEADS_DEV = 8
WIDTH = HEADS_DEV * HEAD_DIM
SLOTS = 16
TOK = 128
IN_A = 320
OUT_A = 224
QUARTER = ENC // 4
MESH = pl.DeviceIdType.MESH
BF16, F32 = jnp.bfloat16, jnp.float32
VMEM_LIMIT = 60 * 1024 * 1024


class Place:
    def __init__(self):
        self.dp, self.group = lax.axis_index("dp"), lax.axis_index("group")
        self.x, self.z = self.group // NZ, self.group % NZ
        self.y, self.core = self.dp // 2, self.dp % 2

    def at_x(self, step):
        return (self.dp, (self.x + step) % NX * NZ + self.z)

    def at_z(self, step):
        return (self.dp, self.x * NZ + (self.z + step) % NZ)

    def at_y(self, step, other=False):
        return ((self.y + step) % NY * 2 + (1 - self.core if other else self.core), self.group)

    def sibling(self):
        return (self.y * 2 + 1 - self.core, self.group)


def meet(peers):
    barrier = pltpu.get_barrier_semaphore()
    for peer in peers:
        pl.semaphore_signal(barrier, inc=1, device_id=peer, device_id_type=MESH)
    pl.semaphore_wait(barrier, len(peers))


class Copies:
    def __init__(self, send_sems, recv_sems, local_sems):
        self.send_sems, self.recv_sems, self.local_sems = send_sems, recv_sems, local_sems
        self.remote, self.local = [], []

    def push(self, src, dst, peer):
        at = len(self.remote)
        copy = pltpu.make_async_remote_copy(
            src_ref=src,
            dst_ref=dst,
            send_sem=self.send_sems.at[at],
            recv_sem=self.recv_sems.at[at],
            device_id=peer,
            device_id_type=MESH,
        )
        copy.start()
        self.remote.append(copy)
        return copy

    def move(self, src, dst):
        copy = pltpu.make_async_copy(src, dst, self.local_sems.at[len(self.local)])
        copy.start()
        self.local.append(copy)
        return copy


def cols(index, width):
    return pl.ds(pl.multiple_of(index * width, width), width)


def dot(a, b, da=1, db=0):
    return lax.dot_general(a, b, (((da,), (db,)), ((), ())), preferred_element_type=F32)


class Gather:
    def __init__(self, run, me, view, rows, cut):
        self.run, self.me, self.view, self.arrived = run, me, view, {}
        self.parts = {1: pl.ds(0, cut), -1: pl.ds(cut, rows - cut)}

    def send(self, hop, way, source=None):
        if hop > 0:
            self.arrived[way, hop - 1].wait_recv()
        block = (self.me.z - way * hop + NZ) % NZ
        there = self.view(block)
        here = there if source is None else source
        if hop == 3:
            here, there = here.at[self.parts[way]], there.at[self.parts[way]]
        self.arrived[way, hop] = self.run.push(here, there, self.me.at_z(way))
        return block

    def end(self):
        for way in (1, -1):
            self.arrived[way, 3].wait_recv()


class Reduce:
    def __init__(self, run, me, own, landed, rows, cut):
        self.run, self.me, self.own, self.landed, self.arrived = run, me, own, landed, {}
        self.parts = {1: pl.ds(0, cut), -1: pl.ds(cut, rows - cut)}

    def send(self, hop, way):
        lane = (1 - way) // 2
        own = self.own((self.me.z + way * (4 - hop) + NZ) % NZ)
        part, rest = self.parts[way], self.parts[-way]
        there = self.landed.at[lane, hop]
        if hop == 0:
            source, there = own.at[part], there.at[part]
        else:
            self.arrived[way, hop - 1].wait_recv()
            source = self.landed.at[lane, hop - 1]
            if hop == 1:
                source[part] = (source[part].astype(F32) + own[part].astype(F32)).astype(BF16)
                source[rest] = own[rest]
            else:
                source[...] = (source[...].astype(F32) + own[...].astype(F32)).astype(BF16)
        self.arrived[way, hop] = self.run.push(source, there, self.me.at_z(way))

    def end(self):
        for way in (1, -1):
            self.arrived[way, 3].wait_recv()
        own = self.own(self.me.z)[...].astype(F32)
        return own + self.landed[0, 3].astype(F32) + self.landed[1, 3].astype(F32)


PUSHES, MOVES = 168, 8


def whole_kernel(
    q_ref, g_ref, enc_ref, kw_ref, vw_ref, ids_ref,
    out_q, ids_all, out_enc, out_w,
    q_x, g_x, enc_all, w_all, ids, table, enc_sel, w_t, kv_t, slots_t, scores, grads, score_bf, weight_bf, qg,
    slot_grads, part_a, part_b, w_part, w_pair, w_sum, land_a, land_b, land_w, x_b, b_sum, a_sum, x_a, y_sum, y_land, y_all,
    send_sems, recv_sems, local_sems
):
    me = Place()
    x, z, core = me.x, me.z, me.core
    scale = HEAD_DIM ** (-0.5)
    meet(
        [me.at_x(1), me.at_x(2), me.at_x(3), me.at_z(1), me.at_z(NZ - 1), me.sibling()]
        + [me.at_y(step) for step in range(1, NY)]
        + [me.at_y(step, other=True) for step in range(1, NY)]
    )
    run = Copies(send_sems, recv_sems, local_sems)
    late = []

    in_a, in_b = pl.ds(0, IN_A), pl.ds(IN_A, ENC - IN_A)
    run.move(ids_ref, ids_all.at[x])
    own_enc = run.move(enc_ref, enc_all.at[x, z])
    quarter = quarter_of(me.y)
    own_w = [
        pltpu.make_async_copy(ref.at[quarter], w_all.at[core, quarter, cols(z, TOK)], local_sems.at[MOVES])
        for ref in (kw_ref, vw_ref)
    ]
    for kind in range(2):
        pl.when(core == kind)(own_w[kind].start)
    gather_b = Gather(run, me, lambda block: enc_all.at[x, block, in_b], ENC - IN_A, 64)
    gather_w = Gather(run, me, lambda block: w_all.at[core, quarter, cols(block, TOK)], QUARTER, 64)
    gathers_a = [
        Gather(run, me, lambda block, chunk=chunk: enc_all.at[(x + chunk) % NX, block, in_a], IN_A, 160)
        for chunk in range(NX)
    ]

    def both_ways(gather, hop, source=None):
        for way in (1, -1):
            gather.send(hop, way, source)

    both_ways(gather_b, 0, enc_ref.at[in_b])
    from_x = {}
    for step in (1, 3, 2):
        from_x[NX - step] = run.push(enc_ref.at[in_a], enc_all.at[x, z, in_a], me.at_x(step))
    lists = [run.push(ids_ref, ids_all.at[x], me.at_x(step)) for step in (1, 2, 3)]
    own_w[0].wait()
    both_ways(gather_w, 0)
    both_ways(gathers_a[0], 0, enc_ref.at[in_a])
    inputs_x = {step: [] for step in range(NX)}

    def exchange(src, dst):
        for step in (1, 3, 2):
            copy = run.push(src.at[:, cols((x + step) % NX, WIDTH)], dst.at[x], me.at_x(step))
            inputs_x[NX - step].append(copy)

    exchange(q_ref, q_x)
    own_inputs = [run.move(src.at[:, cols(x, WIDTH)], dst.at[x]) for src, dst in ((q_ref, q_x), (g_ref, g_x))]
    own_enc.wait()
    both_ways(gather_b, 1)
    both_ways(gather_w, 1)
    for chunk in (1, 3):
        from_x[chunk].wait_recv()
        both_ways(gathers_a[chunk], 0)
    both_ways(gather_b, 2)
    both_ways(gather_w, 2)
    from_x[2].wait_recv()
    both_ways(gathers_a[2], 0)
    both_ways(gather_b, 3)
    both_ways(gather_w, 3)
    both_ways(gathers_a[0], 1)
    gather_b.end()
    blocks_b = enc_all.at[x, :, in_b]
    from_x_b = [run.push(blocks_b, blocks_b, me.at_x(step)) for step in (1, 3, 2)]
    exchange(g_ref, g_x)
    gather_w.end()
    own_quarter = w_all.at[core, quarter]
    from_y = [run.push(own_quarter, own_quarter, me.at_y(step)) for step in (1, NY - 1, 2)]
    from_sibling = [run.push(own_quarter, own_quarter, me.sibling())]
    for chunk in (1, 3, 2):
        both_ways(gathers_a[chunk], 1)
    for chunk in (0, 1, 3, 2):
        both_ways(gathers_a[chunk], 2)
    for copy, step in zip(from_y, (3, 1, 2)):
        copy.wait_recv()
        view = w_all.at[core, quarter_of(me.y + step)]
        from_sibling.append(run.push(view, view, me.sibling()))
    for copy in lists:
        copy.wait_recv()
    run.local[0].wait()
    run.move(ids_all, ids).wait()

    def id_of(slot):
        return ids[slot // 4, slot // 2 % 2, slot % 2] & (NX * NZ - 1)

    def first_of(neighbour, after):
        first = SLOTS
        for slot in range(SLOTS - 1, after, -1):
            first = jnp.where(id_of(slot) == neighbour, slot, first)
        return first

    def fill_table(start):
        @pl.loop(start, start + NZ)
        def _(neighbour):
            table[neighbour] = first_of(neighbour, -1)

    fill_table(0)
    for turn, chunk in enumerate((0, 1, 3, 2)):
        both_ways(gathers_a[chunk], 3)
        if turn < 3:
            fill_table((turn + 1) * NZ)
    for slot in range(SLOTS):
        table[NX * NZ + slot] = first_of(id_of(slot), slot)
    for copy in from_sibling:
        copy.wait_recv()
    for kind in range(2):
        for head in range(HEADS_DEV):
            at = kind * WIDTH + head * HEAD_DIM
            w_t[at : at + HEAD_DIM, :] = w_all[kind, :, head * HEAD_DIM : (head + 1) * HEAD_DIM].T
    slot_grads[SLOTS] = jnp.zeros((ENC, NLEN), BF16)
    for chunk in (0, 1, 3, 2):
        gathers_a[chunk].end()
    for copy in from_x_b:
        copy.wait_recv()

    for slot in range(SLOTS):
        neighbour = id_of(slot)
        enc_sel[:, slot * NLEN : (slot + 1) * NLEN] = enc_all[neighbour // NZ, neighbour % NZ]

    @pl.loop(0, 8)
    def _(span):
        here = cols(span, 2 * NLEN)
        chosen = enc_sel[:, here]
        for tile in range(4):
            rows = pl.ds(tile * 512, 512)
            kv_t[rows, here] = dot(w_t[rows, :], chosen).astype(BF16)

    for step in (1, 3, 2, 0):
        source = (x + step) % NX
        if step == 0:
            for copy in own_inputs:
                copy.wait()
        else:
            for copy in inputs_x[step]:
                copy.wait_recv()

        @pl.loop(0, 2)
        def _(turn):
            here, rows = cols(source * 2 + turn, 2 * NLEN), cols(turn, SPAN)
            for head in range(HEADS_DEV):
                lanes, tile = pl.ds(head * HEAD_DIM, HEAD_DIM), pl.ds(head * SPAN, SPAN)
                scores[tile, :] = dot(q_x[source, rows, lanes], kv_t[lanes, here])
                grads[tile, :] = dot(g_x[source, rows, lanes], kv_t[pl.ds(WIDTH + head * HEAD_DIM, HEAD_DIM), here])
            expo = scores[...]
            expo = jnp.exp((expo - jnp.max(expo, axis=-1, keepdims=True)) * scale)
            weights = expo * (1.0 / jnp.sum(expo, axis=-1, keepdims=True))
            weight_bf[...] = weights.astype(BF16)
            weight_grad = grads[...]
            row_delta = jnp.sum(weights * weight_grad, axis=-1, keepdims=True)
            score_bf[...] = (weights * (weight_grad - row_delta) * scale).astype(BF16)
            for head in range(HEADS_DEV):
                lanes, tile = pl.ds(head * HEAD_DIM, HEAD_DIM), pl.ds(head * SPAN, SPAN)
                query, grad = q_x[source, rows, lanes], g_x[source, rows, lanes]
                qg[source, rows, lanes] = dot(score_bf[tile, :], kv_t[lanes, here], 1, 1).astype(BF16)
                slots_t[lanes, here] = dot(query, score_bf[tile, :], 0, 0).astype(BF16)
                slots_t[pl.ds(WIDTH + head * HEAD_DIM, HEAD_DIM), here] = dot(grad, weight_bf[tile, :], 0, 0).astype(BF16)

        if step == 0:
            run.move(qg.at[x], out_q.at[x])
        else:
            late.append(run.push(qg.at[source], out_q.at[x], me.at_x(step)))

    def slot_products(rows):
        @pl.loop(0, 8)
        def _(span):
            here = cols(span, 2 * NLEN)
            both = dot(w_all[0, rows, :], slots_t[0:WIDTH, here]) + dot(w_all[1, rows, :], slots_t[WIDTH:, here])
            both = both.astype(BF16)
            slot_grads[2 * span, rows] = both[:, 0:NLEN]
            slot_grads[2 * span + 1, rows] = both[:, NLEN:]

        for slot in range(SLOTS - 2, -1, -1):
            slot_grads[slot, rows] = slot_grads[slot, rows] + slot_grads[table[NX * NZ + slot], rows]

    def neighbour_a(at_x, at_z):
        part_a[at_x, at_z] = slot_grads[table[at_x * NZ + at_z], out_a]

    def sum_b(at_x):
        @pl.loop(0, NZ)
        def _(order):
            part_b[at_x, order] = slot_grads[table[at_x * NZ + (z + 3 + order) % NZ], out_b]

    out_a, out_b = pl.ds(0, OUT_A), pl.ds(OUT_A, ENC - OUT_A)
    reduces_a = [
        Reduce(run, me, lambda block, chunk=chunk: part_a.at[chunk, block], land_a.at[chunk], OUT_A, OUT_A // 2)
        for chunk in range(NX)
    ]
    reduce_b = Reduce(
        run, me, lambda block: b_sum.at[(block - z - 3 + 2 * NZ) % NZ], land_b, ENC - OUT_A, (ENC - OUT_A) // 2
    )
    reduce_w = Reduce(run, me, lambda block: w_sum.at[block], land_w, ENC, ENC // 2)

    def turn_of(reduces, hop):
        for reduce in reduces:
            for way in (1, -1):
                reduce.send(hop, way)

    slot_products(out_a)

    @pl.loop(0, NX)
    def _(at_x):
        neighbour_a(at_x, (z + 4) % NZ)

    turn_of(reduces_a, 0)
    slot_products(out_b)
    half = (ENC - OUT_A) // 2
    low, high = pl.ds(0, half), pl.ds(half, half)
    far, right, left = (x + 2) % NX, (x + 1) % NX, (x + 3) % NX
    groups = [pl.ds(0, 3), pl.ds(3, 5)]
    sum_b(far)
    sum_b(right)
    sum_b(left)
    via_left, via_right, high_left, low_right = [], [], [], []
    for group in groups:
        via_left.append(run.push(part_b.at[far, group, low], x_b.at[0, group], me.at_x(1)))
        via_right.append(run.push(part_b.at[far, group, high], x_b.at[1, group], me.at_x(3)))
        high_left.append(run.push(part_b.at[right, group, high], x_b.at[2, group], me.at_x(1)))
        low_right.append(run.push(part_b.at[left, group, low], x_b.at[3, group], me.at_x(3)))

    @pl.loop(0, NX * (NZ - 1))
    def _(turn):
        neighbour_a(turn % NX, (z + 5 + turn // NX) % NZ)

    turn_of(reduces_a, 1)

    def weight_products(kind):
        @pl.loop(0, 4)
        def _(tile):
            rows = pl.ds(pl.multiple_of(kind * WIDTH + tile * 256, 256), 256)
            product = dot(enc_sel[...], slots_t[rows, :], 1, 1).astype(BF16)
            w_part[kind, 2 * tile] = product[:, 0:TOK]
            w_part[kind, 2 * tile + 1] = product[:, TOK:]

    weight_products(1 - core)
    from_sibling = run.push(w_part.at[1 - core], w_pair, me.sibling())
    sum_b(x)
    weight_products(core)

    def add_on(target, landed, rows, group):
        @pl.loop(*group)
        def _(block):
            landed[block] = (landed[block].astype(F32) + part_b[target, block, rows].astype(F32)).astype(BF16)

    low_left, high_right = [], []

    def pass_on(turn):
        group, bounds = groups[turn], ((0, 3), (3, 8))[turn]
        via_left[turn].wait_recv()
        add_on(right, x_b.at[0], low, bounds)
        low_left.append(run.push(x_b.at[0, group], x_b.at[4, group], me.at_x(1)))
        via_right[turn].wait_recv()
        add_on(left, x_b.at[1], high, bounds)
        high_right.append(run.push(x_b.at[1, group], x_b.at[5, group], me.at_x(3)))

    def end_x(turn):
        for copies in (high_left, low_right, low_left, high_right):
            copies[turn].wait_recv()

        @pl.loop(*((0, 3), (3, 8))[turn])
        def _(block):
            for rows, first, second in ((low, 3, 4), (high, 2, 5)):
                total = part_b[x, block, rows].astype(F32) + x_b[first, block].astype(F32)
                b_sum[block, rows] = (total + x_b[second, block].astype(F32)).astype(BF16)

    pass_on(0)
    from_sibling.wait_recv()

    @pl.loop(0, NZ)
    def _(block):
        w_sum[block] = (w_part[core, block].astype(F32) + w_pair[block].astype(F32)).astype(BF16)

    turn_of([reduce_w], 0)
    turn_of(reduces_a, 2)
    turn_of([reduce_w], 1)
    pass_on(1)
    turn_of(reduces_a[:2], 3)
    turn_of([reduce_w], 2)
    turn_of(reduces_a[2:], 3)
    end_x(0)
    turn_of([reduce_b], 0)
    turn_of([reduce_w], 3)
    turn_of([reduce_b], 1)
    from_x = {}
    for chunk in range(NX):
        a_sum[chunk] = reduces_a[chunk].end().astype(BF16)
    for step in (1, 3, 2):
        from_x[step] = run.push(a_sum.at[(x + step) % NX], x_a.at[step - 1], me.at_x(step))
    y = me.y
    y_sum[pl.ds(0, ENC)] = reduce_w.end().astype(BF16)
    y_sum[pl.ds(ENC, 64)] = jnp.zeros((64, TOK), BF16)
    from_y = []
    for step in range(1, NY):
        from_y.append(run.push(y_sum.at[rows_of((y + step) % NY)], y_land.at[step - 1], me.at_y(step)))
    end_x(1)
    turn_of([reduce_b], 2)
    total = y_sum[rows_of(y)].astype(F32)
    for step in range(1, NY):
        from_y[step - 1].wait_recv()
        total += y_land[step - 1].astype(F32)
    y_all[core, rows_of(y)] = total.astype(BF16)
    own_rows = y_all.at[core, rows_of(y)]
    from_y = [run.push(own_rows, own_rows, me.at_y(step)) for step in range(1, NY)]
    from_y += [run.push(own_rows, own_rows, me.at_y(step, other=True)) for step in range(NY)]
    turn_of([reduce_b], 3)
    total = a_sum[x].astype(F32)
    for step in (1, 3, 2):
        from_x[step].wait_recv()
        total += x_a[step - 1].astype(F32)
    out_enc[out_a] = total.astype(BF16)
    for copy in from_y:
        copy.wait_recv()
    for kind in range(2):
        out_w[kind] = y_all[kind, pl.ds(0, ENC)].astype(F32)
    out_enc[out_b] = reduce_b.end().astype(BF16)
    for copy in late:
        copy.wait_recv()
    for copy in run.remote:
        copy.wait_send()
    run.local[-1].wait()


def quarter_of(index):
    return pl.ds(pl.multiple_of(index % 4 * QUARTER, QUARTER), QUARTER)


def rows_of(index):
    return pl.ds(pl.multiple_of(index * 64, 64), 64)


def whole(queries, out_grad, enc_t, key_weight, value_weight, ids):
    anywhere, vmem = pl.BlockSpec(memory_space=pl.ANY), pl.BlockSpec(memory_space=pltpu.VMEM)
    enc_b = ENC - OUT_A
    bf = lambda *shape: pltpu.VMEM(shape, BF16)
    f32 = lambda *shape: pltpu.VMEM(shape, F32)
    return pl.pallas_call(
        whole_kernel,
        out_shape=[
            jax.ShapeDtypeStruct((NX, TOK, WIDTH), BF16),
            jax.ShapeDtypeStruct((NX, 2, 2), jnp.int32),
            jax.ShapeDtypeStruct((ENC, NLEN), BF16),
            jax.ShapeDtypeStruct((2, ENC, TOK), F32),
        ],
        in_specs=[anywhere] * 6,
        out_specs=[anywhere, anywhere, vmem, vmem],
        scratch_shapes=[
            bf(NX, TOK, WIDTH),
            bf(NX, TOK, WIDTH),
            bf(NX, NZ, ENC, NLEN),
            bf(2, ENC, WIDTH),
            pltpu.SMEM((NX, 2, 2), jnp.int32),
            pltpu.SMEM((NX * NZ + SLOTS,), jnp.int32),
            bf(ENC, SLOTS * NLEN),
            bf(2 * WIDTH, ENC),
            bf(2 * WIDTH, SLOTS * NLEN),
            bf(2 * WIDTH, SLOTS * NLEN),
            f32(HEADS_DEV * SPAN, 2 * NLEN),
            f32(HEADS_DEV * SPAN, 2 * NLEN),
            bf(HEADS_DEV * SPAN, 2 * NLEN),
            bf(HEADS_DEV * SPAN, 2 * NLEN),
            bf(NX, TOK, WIDTH),
            bf(SLOTS + 1, ENC, NLEN),
            bf(NX, NZ, OUT_A, NLEN),
            bf(NX, NZ, enc_b, NLEN),
            bf(2, NZ, ENC, TOK),
            bf(NZ, ENC, TOK),
            bf(NZ, ENC, TOK),
            bf(NX, 2, 4, OUT_A, NLEN),
            bf(2, 4, enc_b, NLEN),
            bf(2, 4, ENC, TOK),
            bf(6, NZ, enc_b // 2, NLEN),
            bf(NZ, enc_b, NLEN),
            bf(NX, OUT_A, NLEN),
            bf(NX - 1, OUT_A, NLEN),
            bf(512, TOK),
            bf(NY - 1, 64, TOK),
            bf(2, 512, TOK),
            pltpu.SemaphoreType.DMA((PUSHES,)),
            pltpu.SemaphoreType.DMA((PUSHES,)),
            pltpu.SemaphoreType.DMA((MOVES + 1,)),
        ],
        compiler_params=pltpu.CompilerParams(collective_id=0, has_side_effects=True, vmem_limit_bytes=VMEM_LIMIT),
    )(queries, out_grad, enc_t, key_weight, value_weight, ids)


def close_kernel(q_ref, enc_ref, w_ref, out_q, out_enc, out_k, out_v, sems):
    copies = [
        pltpu.make_async_copy(q_ref.at[source], out_q.at[:, pl.ds(source * WIDTH, WIDTH)], sems.at[source])
        for source in range(NX)
    ]
    copies.append(pltpu.make_async_copy(enc_ref, out_enc, sems.at[4]))
    copies.append(pltpu.make_async_copy(w_ref.at[0], out_k, sems.at[5]))
    copies.append(pltpu.make_async_copy(w_ref.at[1], out_v, sems.at[6]))
    for copy in copies:
        copy.start()
    for copy in copies:
        copy.wait()


def close(query_grads, enc_grad, weight_grads):
    anywhere, vmem = pl.BlockSpec(memory_space=pl.ANY), pl.BlockSpec(memory_space=pltpu.VMEM)
    return pl.pallas_call(
        close_kernel,
        out_shape=[
            jax.ShapeDtypeStruct((TOK, NX * WIDTH), BF16),
            jax.ShapeDtypeStruct((ENC, NLEN), BF16),
            jax.ShapeDtypeStruct((ENC, TOK), F32),
            jax.ShapeDtypeStruct((ENC, TOK), F32),
        ],
        in_specs=[anywhere] * 3,
        out_specs=[vmem] * 4,
        scratch_shapes=[pltpu.SemaphoreType.DMA((7,))],
        compiler_params=pltpu.CompilerParams(vmem_limit_bytes=VMEM_LIMIT),
    )(query_grads, enc_grad, weight_grads)


def local(queries, out_grad, encodings, key_weight, value_weight, nbr_ids):
    enc_t = jnp.swapaxes(encodings[0], 0, 1)
    query_grads, _, enc_grad, weight_grads = whole(queries, out_grad, enc_t, key_weight, value_weight, nbr_ids)
    query_grad, enc_grad, key_grad, value_grad = close(query_grads, enc_grad, weight_grads)
    return query_grad, jnp.swapaxes(enc_grad, 0, 1)[None], key_grad, value_grad


def solution(mesh):
    in_specs = (
        P(("dp", "group"), None),
        P(("dp", "group"), None),
        P(("dp", "group"), None, None),
        P(None, "group"),
        P(None, "group"),
        P(("dp", "group"), None),
    )
    out_specs = (
        P(("dp", "group"), None),
        P(("dp", "group"), None, None),
        P(None, "group"),
        P(None, "group"),
    )
    return jax.shard_map(local, mesh=mesh, in_specs=in_specs, out_specs=out_specs, check_vma=False)
```

```python
import functools

import jax
import jax.numpy as jnp
from jax import lax
from jax.experimental import pallas as pl
from jax.experimental.pallas import tpu as pltpu
from jax.sharding import PartitionSpec as P

HEAD_DIM = 128
SPAN = 64
NLEN = 128
ENC = 448
NX, NZ, NY = 4, 8, 8
HEADS_DEV = 8
WIDTH = HEADS_DEV * HEAD_DIM
SLOTS = 16
TOK = 128
IN_A = 320
OUT_A = 160
QUARTER = ENC // 4
MESH = pl.DeviceIdType.MESH
BF16, F32 = jnp.bfloat16, jnp.float32
VMEM_LIMIT = 60 * 1024 * 1024


class Place:
    def __init__(self):
        self.dp, self.group = lax.axis_index("dp"), lax.axis_index("group")
        self.x, self.z = self.group // NZ, self.group % NZ
        self.y, self.core = self.dp // 2, self.dp % 2

    def at_x(self, step):
        return (self.dp, (self.x + step) % NX * NZ + self.z)

    def at_z(self, step):
        return (self.dp, self.x * NZ + (self.z + step) % NZ)

    def at_y(self, step, other=False):
        return ((self.y + step) % NY * 2 + (1 - self.core if other else self.core), self.group)

    def sibling(self):
        return (self.y * 2 + 1 - self.core, self.group)


def meet(peers):
    barrier = pltpu.get_barrier_semaphore()
    for peer in peers:
        pl.semaphore_signal(barrier, inc=1, device_id=peer, device_id_type=MESH)
    pl.semaphore_wait(barrier, len(peers))


class Copies:
    def __init__(self, send_sems, recv_sems, local_sems):
        self.send_sems, self.recv_sems, self.local_sems = send_sems, recv_sems, local_sems
        self.remote, self.local = [], []

    def push(self, src, dst, peer):
        at = len(self.remote)
        copy = pltpu.make_async_remote_copy(
            src_ref=src,
            dst_ref=dst,
            send_sem=self.send_sems.at[at],
            recv_sem=self.recv_sems.at[at],
            device_id=peer,
            device_id_type=MESH,
        )
        copy.start()
        self.remote.append(copy)
        return copy

    def move(self, src, dst):
        copy = pltpu.make_async_copy(src, dst, self.local_sems.at[len(self.local)])
        copy.start()
        self.local.append(copy)
        return copy


def cols(index, width):
    return pl.ds(pl.multiple_of(index * width, width), width)


def dot(a, b, da=1, db=0):
    return lax.dot_general(a, b, (((da,), (db,)), ((), ())), preferred_element_type=F32)


class Gather:
    def __init__(self, run, me, view, rows, cut):
        self.run, self.me, self.view, self.arrived = run, me, view, {}
        self.parts = {1: pl.ds(0, cut), -1: pl.ds(cut, rows - cut)}

    def send(self, hop, way, source=None):
        if hop > 0:
            self.arrived[way, hop - 1].wait_recv()
        block = (self.me.z - way * hop + NZ) % NZ
        there = self.view(block)
        here = there if source is None else source
        if hop == 3:
            here, there = here.at[self.parts[way]], there.at[self.parts[way]]
        self.arrived[way, hop] = self.run.push(here, there, self.me.at_z(way))
        return block

    def end(self):
        for way in (1, -1):
            self.arrived[way, 3].wait_recv()


class Reduce:
    def __init__(self, run, me, own, landed, rows, cut):
        self.run, self.me, self.own, self.landed, self.arrived = run, me, own, landed, {}
        self.parts = {1: pl.ds(0, cut), -1: pl.ds(cut, rows - cut)}

    def send(self, hop, way):
        lane = (1 - way) // 2
        own = self.own((self.me.z + way * (4 - hop) + NZ) % NZ)
        part, rest = self.parts[way], self.parts[-way]
        there = self.landed.at[lane, hop]
        if hop == 0:
            source, there = own.at[part], there.at[part]
        else:
            self.arrived[way, hop - 1].wait_recv()
            source = self.landed.at[lane, hop - 1]
            if hop == 1:
                source[part] = (source[part].astype(F32) + own[part].astype(F32)).astype(BF16)
                source[rest] = own[rest]
            else:
                source[...] = (source[...].astype(F32) + own[...].astype(F32)).astype(BF16)
        self.arrived[way, hop] = self.run.push(source, there, self.me.at_z(way))

    def end(self):
        for way in (1, -1):
            self.arrived[way, 3].wait_recv()
        own = self.own(self.me.z)[...].astype(F32)
        return own + self.landed[0, 3].astype(F32) + self.landed[1, 3].astype(F32)


PUSHES, MOVES = 168, 8
ORDER = (
    "w_other", "w_own", "w_pair_up", "w0", "b_products", "b_over_x",
    "w1", "a_products", "a_first", "a0", "a_rest", "w2",
    "b_own", "b_pass_on_0", "a1", "w3", "b_pass_on_1", "a2",
    "w_over_y", "b_sum_up_0", "b0", "a3", "w_hand_on", "b1",
    "a_over_x", "b_sum_up_1", "b2", "a_end", "w_end", "b3",
    "b_end",
)


def whole_kernel(
    q_ref, g_ref, enc_ref, kw_ref, vw_ref, ids_ref,
    out_q, ids_all, out_enc, out_w,
    q_x, g_x, enc_all, w_all, ids, table, enc_sel, w_t, kv_t, slots_t, scores, grads, score_bf, weight_bf, qg,
    slot_grads, part_a, part_b, w_part, w_pair, w_sum, land_a, land_b, land_w, x_b, b_sum, a_sum, x_a, y_sum, y_land, y_all,
    send_sems, recv_sems, local_sems
):
    me = Place()
    x, z, core = me.x, me.z, me.core
    scale = HEAD_DIM ** (-0.5)
    meet(
        [me.at_x(1), me.at_x(2), me.at_x(3), me.at_z(1), me.at_z(NZ - 1), me.sibling()]
        + [me.at_y(step) for step in range(1, NY)]
        + [me.at_y(step, other=True) for step in range(1, NY)]
    )
    run = Copies(send_sems, recv_sems, local_sems)
    late = []

    in_a, in_b = pl.ds(0, IN_A), pl.ds(IN_A, ENC - IN_A)
    run.move(ids_ref, ids_all.at[x])
    own_enc = run.move(enc_ref, enc_all.at[x, z])
    quarter = quarter_of(me.y)
    own_w = [
        pltpu.make_async_copy(ref.at[quarter], w_all.at[core, quarter, cols(z, TOK)], local_sems.at[MOVES])
        for ref in (kw_ref, vw_ref)
    ]
    for kind in range(2):
        pl.when(core == kind)(own_w[kind].start)
    gather_b = Gather(run, me, lambda block: enc_all.at[x, block, in_b], ENC - IN_A, 64)
    gather_w = Gather(run, me, lambda block: w_all.at[core, quarter, cols(block, TOK)], QUARTER, 64)
    gathers_a = [
        Gather(run, me, lambda block, chunk=chunk: enc_all.at[(x + chunk) % NX, block, in_a], IN_A, 160)
        for chunk in range(NX)
    ]

    def both_ways(gather, hop, source=None):
        for way in (1, -1):
            gather.send(hop, way, source)

    both_ways(gather_b, 0, enc_ref.at[in_b])
    from_x = {}
    for step in (1, 3, 2):
        from_x[NX - step] = run.push(enc_ref.at[in_a], enc_all.at[x, z, in_a], me.at_x(step))
    lists = [run.push(ids_ref, ids_all.at[x], me.at_x(step)) for step in (1, 2, 3)]
    own_w[0].wait()
    both_ways(gather_w, 0)
    both_ways(gathers_a[0], 0, enc_ref.at[in_a])
    inputs_x = {step: [] for step in range(NX)}

    def exchange(src, dst):
        for step in (1, 3, 2):
            copy = run.push(src.at[:, cols((x + step) % NX, WIDTH)], dst.at[x], me.at_x(step))
            inputs_x[NX - step].append(copy)

    exchange(q_ref, q_x)
    own_inputs = [run.move(src.at[:, cols(x, WIDTH)], dst.at[x]) for src, dst in ((q_ref, q_x), (g_ref, g_x))]
    own_enc.wait()
    both_ways(gather_b, 1)
    both_ways(gather_w, 1)
    for chunk in (1, 3):
        from_x[chunk].wait_recv()
        both_ways(gathers_a[chunk], 0)
    both_ways(gather_b, 2)
    both_ways(gather_w, 2)
    from_x[2].wait_recv()
    both_ways(gathers_a[2], 0)
    both_ways(gather_b, 3)
    both_ways(gather_w, 3)
    both_ways(gathers_a[0], 1)
    gather_b.end()
    blocks_b = enc_all.at[x, :, in_b]
    from_x_b = [run.push(blocks_b, blocks_b, me.at_x(step)) for step in (1, 3, 2)]
    exchange(g_ref, g_x)
    gather_w.end()
    own_quarter = w_all.at[core, quarter]
    from_y = [run.push(own_quarter, own_quarter, me.at_y(step)) for step in (1, NY - 1, 2)]
    from_sibling = [run.push(own_quarter, own_quarter, me.sibling())]
    for chunk in (1, 3, 2):
        both_ways(gathers_a[chunk], 1)
    for chunk in (0, 1, 3, 2):
        both_ways(gathers_a[chunk], 2)
    for copy, step in zip(from_y, (3, 1, 2)):
        copy.wait_recv()
        view = w_all.at[core, quarter_of(me.y + step)]
        from_sibling.append(run.push(view, view, me.sibling()))
    for copy in lists:
        copy.wait_recv()
    run.local[0].wait()
    run.move(ids_all, ids).wait()

    def id_of(slot):
        return ids[slot // 4, slot // 2 % 2, slot % 2] & (NX * NZ - 1)

    def first_of(neighbour, after):
        first = SLOTS
        for slot in range(SLOTS - 1, after, -1):
            first = jnp.where(id_of(slot) == neighbour, slot, first)
        return first

    def fill_table(start):
        @pl.loop(start, start + NZ)
        def _(neighbour):
            table[neighbour] = first_of(neighbour, -1)

    fill_table(0)
    for turn, chunk in enumerate((0, 1, 3, 2)):
        both_ways(gathers_a[chunk], 3)
        if turn < 3:
            fill_table((turn + 1) * NZ)
    for slot in range(SLOTS):
        table[NX * NZ + slot] = first_of(id_of(slot), slot)
    for copy in from_sibling:
        copy.wait_recv()
    for kind in range(2):
        for head in range(HEADS_DEV):
            at = kind * WIDTH + head * HEAD_DIM
            w_t[at : at + HEAD_DIM, :] = w_all[kind, :, head * HEAD_DIM : (head + 1) * HEAD_DIM].T
    slot_grads[SLOTS] = jnp.zeros((ENC, NLEN), BF16)
    for chunk in (0, 1, 3, 2):
        gathers_a[chunk].end()
    for copy in from_x_b:
        copy.wait_recv()

    for slot in range(SLOTS):
        neighbour = id_of(slot)
        enc_sel[:, slot * NLEN : (slot + 1) * NLEN] = enc_all[neighbour // NZ, neighbour % NZ]

    @pl.loop(0, 8)
    def _(span):
        here = cols(span, 2 * NLEN)
        chosen = enc_sel[:, here]
        for tile in range(4):
            rows = pl.ds(tile * 512, 512)
            kv_t[rows, here] = dot(w_t[rows, :], chosen).astype(BF16)

    for step in (1, 3, 2, 0):
        source = (x + step) % NX
        if step == 0:
            for copy in own_inputs:
                copy.wait()
        else:
            for copy in inputs_x[step]:
                copy.wait_recv()

        @pl.loop(0, 2)
        def _(turn):
            here, rows = cols(source * 2 + turn, 2 * NLEN), cols(turn, SPAN)
            for head in range(HEADS_DEV):
                lanes, tile = pl.ds(head * HEAD_DIM, HEAD_DIM), pl.ds(head * SPAN, SPAN)
                scores[tile, :] = dot(q_x[source, rows, lanes], kv_t[lanes, here])
                grads[tile, :] = dot(g_x[source, rows, lanes], kv_t[pl.ds(WIDTH + head * HEAD_DIM, HEAD_DIM), here])
            expo = scores[...]
            expo = jnp.exp((expo - jnp.max(expo, axis=-1, keepdims=True)) * scale)
            weights = expo * (1.0 / jnp.sum(expo, axis=-1, keepdims=True))
            weight_bf[...] = weights.astype(BF16)
            weight_grad = grads[...]
            row_delta = jnp.sum(weights * weight_grad, axis=-1, keepdims=True)
            score_bf[...] = (weights * (weight_grad - row_delta) * scale).astype(BF16)
            for head in range(HEADS_DEV):
                lanes, tile = pl.ds(head * HEAD_DIM, HEAD_DIM), pl.ds(head * SPAN, SPAN)
                query, grad = q_x[source, rows, lanes], g_x[source, rows, lanes]
                qg[source, rows, lanes] = dot(score_bf[tile, :], kv_t[lanes, here], 1, 1).astype(BF16)
                slots_t[lanes, here] = dot(query, score_bf[tile, :], 0, 0).astype(BF16)
                slots_t[pl.ds(WIDTH + head * HEAD_DIM, HEAD_DIM), here] = dot(grad, weight_bf[tile, :], 0, 0).astype(BF16)

        if step == 0:
            run.move(qg.at[x], out_q.at[x])
        else:
            late.append(run.push(qg.at[source], out_q.at[x], me.at_x(step)))

    def slot_products(rows):
        @pl.loop(0, 8)
        def _(span):
            here = cols(span, 2 * NLEN)
            both = dot(w_all[0, rows, :], slots_t[0:WIDTH, here]) + dot(w_all[1, rows, :], slots_t[WIDTH:, here])
            both = both.astype(BF16)
            slot_grads[2 * span, rows] = both[:, 0:NLEN]
            slot_grads[2 * span + 1, rows] = both[:, NLEN:]

        for slot in range(SLOTS - 2, -1, -1):
            slot_grads[slot, rows] = slot_grads[slot, rows] + slot_grads[table[NX * NZ + slot], rows]

    def neighbour_a(at_x, at_z):
        part_a[at_x, at_z] = slot_grads[table[at_x * NZ + at_z], out_a]

    def sum_b(at_x):
        @pl.loop(0, NZ)
        def _(order):
            part_b[at_x, order] = slot_grads[table[at_x * NZ + (z + 3 + order) % NZ], out_b]

    out_a, out_b = pl.ds(0, OUT_A), pl.ds(OUT_A, ENC - OUT_A)
    half = (ENC - OUT_A) // 2
    low, high = pl.ds(0, half), pl.ds(half, half)
    far, right, left = (x + 2) % NX, (x + 1) % NX, (x + 3) % NX
    groups, bounds = [pl.ds(0, 3), pl.ds(3, 5)], [(0, 3), (3, 8)]
    y = me.y
    going = {}
    reduces_a = [
        Reduce(run, me, lambda block, chunk=chunk: part_a.at[chunk, block], land_a.at[chunk], OUT_A, OUT_A // 2)
        for chunk in range(NX)
    ]
    reduce_b = Reduce(run, me, lambda block: b_sum.at[(block - z - 3 + 2 * NZ) % NZ], land_b, ENC - OUT_A, half)
    reduce_w = Reduce(run, me, lambda block: w_sum.at[block], land_w, ENC, ENC // 2)

    def turn(reduces, hop):
        for reduce in reduces:
            for way in (1, -1):
                reduce.send(hop, way)

    def a_first():
        @pl.loop(0, NX)
        def _(at_x):
            neighbour_a(at_x, (z + 4) % NZ)

    def a_rest():
        @pl.loop(0, NX * (NZ - 1))
        def _(index):
            neighbour_a(index % NX, (z + 5 + index // NX) % NZ)

    def a_over_x():
        for chunk in range(NX):
            a_sum[chunk] = reduces_a[chunk].end().astype(BF16)
        going["a"] = [run.push(a_sum.at[(x + step) % NX], x_a.at[step - 1], me.at_x(step)) for step in (1, 2, 3)]

    def a_end():
        total = a_sum[x].astype(F32)
        for step in range(NX - 1):
            going["a"][step].wait_recv()
            total += x_a[step].astype(F32)
        out_enc[out_a] = total.astype(BF16)

    def b_over_x():
        for at_x in (far, right, left):
            sum_b(at_x)
        going["b"] = []
        for group in groups:
            via_left = run.push(part_b.at[far, group, low], x_b.at[0, group], me.at_x(1))
            via_right = run.push(part_b.at[far, group, high], x_b.at[1, group], me.at_x(3))
            high_left = run.push(part_b.at[right, group, high], x_b.at[2, group], me.at_x(1))
            low_right = run.push(part_b.at[left, group, low], x_b.at[3, group], me.at_x(3))
            going["b"].append([via_left, via_right, high_left, low_right])

    def add_on(target, landed, rows, blocks):
        @pl.loop(*blocks)
        def _(block):
            landed[block] = (landed[block].astype(F32) + part_b[target, block, rows].astype(F32)).astype(BF16)

    def b_pass_on(at):
        group, copies = groups[at], going["b"][at]
        copies[0].wait_recv()
        add_on(right, x_b.at[0], low, bounds[at])
        copies[0] = run.push(x_b.at[0, group], x_b.at[4, group], me.at_x(1))
        copies[1].wait_recv()
        add_on(left, x_b.at[1], high, bounds[at])
        copies[1] = run.push(x_b.at[1, group], x_b.at[5, group], me.at_x(3))

    def b_sum_up(at):
        for copy in going["b"][at]:
            copy.wait_recv()

        @pl.loop(*bounds[at])
        def _(block):
            for rows, first, second in ((low, 3, 4), (high, 2, 5)):
                total = part_b[x, block, rows].astype(F32) + x_b[first, block].astype(F32)
                b_sum[block, rows] = (total + x_b[second, block].astype(F32)).astype(BF16)

    def b_end():
        out_enc[out_b] = reduce_b.end().astype(BF16)

    def weight_products(kind):
        @pl.loop(0, 4)
        def _(tile):
            rows = pl.ds(pl.multiple_of(kind * WIDTH + tile * 256, 256), 256)
            product = dot(enc_sel[...], slots_t[rows, :], 1, 1).astype(BF16)
            w_part[kind, 2 * tile] = product[:, 0:TOK]
            w_part[kind, 2 * tile + 1] = product[:, TOK:]

    def w_other():
        weight_products(1 - core)
        going["pair"] = run.push(w_part.at[1 - core], w_pair, me.sibling())

    def w_pair_up():
        going["pair"].wait_recv()

        @pl.loop(0, NZ)
        def _(block):
            w_sum[block] = (w_part[core, block].astype(F32) + w_pair[block].astype(F32)).astype(BF16)

    def w_over_y():
        y_sum[pl.ds(0, ENC)] = reduce_w.end().astype(BF16)
        y_sum[pl.ds(ENC, 64)] = jnp.zeros((64, TOK), BF16)
        going["y"] = [
            run.push(y_sum.at[rows_of((y + step) % NY)], y_land.at[step - 1], me.at_y(step)) for step in range(1, NY)
        ]

    def w_hand_on():
        total = y_sum[rows_of(y)].astype(F32)
        for step in range(NY - 1):
            going["y"][step].wait_recv()
            total += y_land[step].astype(F32)
        y_all[core, rows_of(y)] = total.astype(BF16)
        own_rows = y_all.at[core, rows_of(y)]
        going["y"] = [run.push(own_rows, own_rows, me.at_y(step)) for step in range(1, NY)]
        going["y"] += [run.push(own_rows, own_rows, me.at_y(step, other=True)) for step in range(NY)]

    def w_end():
        for copy in going["y"]:
            copy.wait_recv()
        for kind in range(2):
            out_w[kind] = y_all[kind, pl.ds(0, ENC)].astype(F32)

    steps = {
        "a_products": lambda: slot_products(out_a),
        "a_first": a_first,
        "a_rest": a_rest,
        "a0": lambda: turn(reduces_a, 0),
        "a1": lambda: turn(reduces_a, 1),
        "a2": lambda: turn(reduces_a, 2),
        "a3": lambda: turn(reduces_a, 3),
        "a_over_x": a_over_x,
        "a_end": a_end,
        "b_products": lambda: slot_products(out_b),
        "b_over_x": b_over_x,
        "b_own": lambda: sum_b(x),
        "b_pass_on_0": lambda: b_pass_on(0),
        "b_pass_on_1": lambda: b_pass_on(1),
        "b_sum_up_0": lambda: b_sum_up(0),
        "b_sum_up_1": lambda: b_sum_up(1),
        "b0": lambda: turn([reduce_b], 0),
        "b1": lambda: turn([reduce_b], 1),
        "b2": lambda: turn([reduce_b], 2),
        "b3": lambda: turn([reduce_b], 3),
        "b_end": b_end,
        "w_other": w_other,
        "w_own": lambda: weight_products(core),
        "w_pair_up": w_pair_up,
        "w0": lambda: turn([reduce_w], 0),
        "w1": lambda: turn([reduce_w], 1),
        "w2": lambda: turn([reduce_w], 2),
        "w3": lambda: turn([reduce_w], 3),
        "w_over_y": w_over_y,
        "w_hand_on": w_hand_on,
        "w_end": w_end,
    }
    for name in ORDER:
        steps[name]()

    for copy in late:
        copy.wait_recv()
    for copy in run.remote:
        copy.wait_send()
    run.local[-1].wait()


def quarter_of(index):
    return pl.ds(pl.multiple_of(index % 4 * QUARTER, QUARTER), QUARTER)


def rows_of(index):
    return pl.ds(pl.multiple_of(index * 64, 64), 64)


def whole(queries, out_grad, enc_t, key_weight, value_weight, ids):
    anywhere, vmem = pl.BlockSpec(memory_space=pl.ANY), pl.BlockSpec(memory_space=pltpu.VMEM)
    enc_b = ENC - OUT_A
    bf = lambda *shape: pltpu.VMEM(shape, BF16)
    f32 = lambda *shape: pltpu.VMEM(shape, F32)
    return pl.pallas_call(
        whole_kernel,
        out_shape=[
            jax.ShapeDtypeStruct((NX, TOK, WIDTH), BF16),
            jax.ShapeDtypeStruct((NX, 2, 2), jnp.int32),
            jax.ShapeDtypeStruct((ENC, NLEN), BF16),
            jax.ShapeDtypeStruct((2, ENC, TOK), F32),
        ],
        in_specs=[anywhere] * 6,
        out_specs=[anywhere, anywhere, vmem, vmem],
        scratch_shapes=[
            bf(NX, TOK, WIDTH),
            bf(NX, TOK, WIDTH),
            bf(NX, NZ, ENC, NLEN),
            bf(2, ENC, WIDTH),
            pltpu.SMEM((NX, 2, 2), jnp.int32),
            pltpu.SMEM((NX * NZ + SLOTS,), jnp.int32),
            bf(ENC, SLOTS * NLEN),
            bf(2 * WIDTH, ENC),
            bf(2 * WIDTH, SLOTS * NLEN),
            bf(2 * WIDTH, SLOTS * NLEN),
            f32(HEADS_DEV * SPAN, 2 * NLEN),
            f32(HEADS_DEV * SPAN, 2 * NLEN),
            bf(HEADS_DEV * SPAN, 2 * NLEN),
            bf(HEADS_DEV * SPAN, 2 * NLEN),
            bf(NX, TOK, WIDTH),
            bf(SLOTS + 1, ENC, NLEN),
            bf(NX, NZ, OUT_A, NLEN),
            bf(NX, NZ, enc_b, NLEN),
            bf(2, NZ, ENC, TOK),
            bf(NZ, ENC, TOK),
            bf(NZ, ENC, TOK),
            bf(NX, 2, 4, OUT_A, NLEN),
            bf(2, 4, enc_b, NLEN),
            bf(2, 4, ENC, TOK),
            bf(6, NZ, enc_b // 2, NLEN),
            bf(NZ, enc_b, NLEN),
            bf(NX, OUT_A, NLEN),
            bf(NX - 1, OUT_A, NLEN),
            bf(512, TOK),
            bf(NY - 1, 64, TOK),
            bf(2, 512, TOK),
            pltpu.SemaphoreType.DMA((PUSHES,)),
            pltpu.SemaphoreType.DMA((PUSHES,)),
            pltpu.SemaphoreType.DMA((MOVES + 1,)),
        ],
        compiler_params=pltpu.CompilerParams(collective_id=0, has_side_effects=True, vmem_limit_bytes=VMEM_LIMIT),
    )(queries, out_grad, enc_t, key_weight, value_weight, ids)


def close_kernel(q_ref, enc_ref, w_ref, out_q, out_enc, out_k, out_v, sems):
    copies = [
        pltpu.make_async_copy(q_ref.at[source], out_q.at[:, pl.ds(source * WIDTH, WIDTH)], sems.at[source])
        for source in range(NX)
    ]
    copies.append(pltpu.make_async_copy(enc_ref, out_enc, sems.at[4]))
    copies.append(pltpu.make_async_copy(w_ref.at[0], out_k, sems.at[5]))
    copies.append(pltpu.make_async_copy(w_ref.at[1], out_v, sems.at[6]))
    for copy in copies:
        copy.start()
    for copy in copies:
        copy.wait()


def close(query_grads, enc_grad, weight_grads):
    anywhere, vmem = pl.BlockSpec(memory_space=pl.ANY), pl.BlockSpec(memory_space=pltpu.VMEM)
    return pl.pallas_call(
        close_kernel,
        out_shape=[
            jax.ShapeDtypeStruct((TOK, NX * WIDTH), BF16),
            jax.ShapeDtypeStruct((ENC, NLEN), BF16),
            jax.ShapeDtypeStruct((ENC, TOK), F32),
            jax.ShapeDtypeStruct((ENC, TOK), F32),
        ],
        in_specs=[anywhere] * 3,
        out_specs=[vmem] * 4,
        scratch_shapes=[pltpu.SemaphoreType.DMA((7,))],
        compiler_params=pltpu.CompilerParams(vmem_limit_bytes=VMEM_LIMIT),
    )(query_grads, enc_grad, weight_grads)


def local(queries, out_grad, encodings, key_weight, value_weight, nbr_ids):
    enc_t = jnp.swapaxes(encodings[0], 0, 1)
    query_grads, _, enc_grad, weight_grads = whole(queries, out_grad, enc_t, key_weight, value_weight, nbr_ids)
    query_grad, enc_grad, key_grad, value_grad = close(query_grads, enc_grad, weight_grads)
    return query_grad, jnp.swapaxes(enc_grad, 0, 1)[None], key_grad, value_grad


def solution(mesh):
    in_specs = (
        P(("dp", "group"), None),
        P(("dp", "group"), None),
        P(("dp", "group"), None, None),
        P(None, "group"),
        P(None, "group"),
        P(("dp", "group"), None),
    )
    out_specs = (
        P(("dp", "group"), None),
        P(("dp", "group"), None, None),
        P(None, "group"),
        P(None, "group"),
    )
    return jax.shard_map(local, mesh=mesh, in_specs=in_specs, out_specs=out_specs, check_vma=False)
```

```python
import functools

import jax
import jax.numpy as jnp
from jax import lax
from jax.experimental import pallas as pl
from jax.experimental.pallas import tpu as pltpu
from jax.sharding import PartitionSpec as P

HEAD_DIM = 128
SPAN = 64
NLEN = 128
ENC = 448
NX, NZ, NY = 4, 8, 8
HEADS_DEV = 8
WIDTH = HEADS_DEV * HEAD_DIM
SLOTS = 16
TOK = 128
IN_A = 288
OUT_A = 160
QUARTER = ENC // 4
MESH = pl.DeviceIdType.MESH
BF16, F32 = jnp.bfloat16, jnp.float32
VMEM_LIMIT = 60 * 1024 * 1024


class Place:
    def __init__(self):
        self.dp, self.group = lax.axis_index("dp"), lax.axis_index("group")
        self.x, self.z = self.group // NZ, self.group % NZ
        self.y, self.core = self.dp // 2, self.dp % 2

    def at_x(self, step):
        return (self.dp, (self.x + step) % NX * NZ + self.z)

    def at_z(self, step):
        return (self.dp, self.x * NZ + (self.z + step) % NZ)

    def at_y(self, step, other=False):
        return ((self.y + step) % NY * 2 + (1 - self.core if other else self.core), self.group)

    def sibling(self):
        return (self.y * 2 + 1 - self.core, self.group)


def meet(peers):
    barrier = pltpu.get_barrier_semaphore()
    for peer in peers:
        pl.semaphore_signal(barrier, inc=1, device_id=peer, device_id_type=MESH)
    pl.semaphore_wait(barrier, len(peers))


class Copies:
    def __init__(self, send_sems, recv_sems, local_sems):
        self.send_sems, self.recv_sems, self.local_sems = send_sems, recv_sems, local_sems
        self.remote, self.local = [], []

    def push(self, src, dst, peer):
        at = len(self.remote)
        copy = pltpu.make_async_remote_copy(
            src_ref=src,
            dst_ref=dst,
            send_sem=self.send_sems.at[at],
            recv_sem=self.recv_sems.at[at],
            device_id=peer,
            device_id_type=MESH,
        )
        copy.start()
        self.remote.append(copy)
        return copy

    def move(self, src, dst):
        copy = pltpu.make_async_copy(src, dst, self.local_sems.at[len(self.local)])
        copy.start()
        self.local.append(copy)
        return copy


def cols(index, width):
    return pl.ds(pl.multiple_of(index * width, width), width)


def dot(a, b, da=1, db=0):
    return lax.dot_general(a, b, (((da,), (db,)), ((), ())), preferred_element_type=F32)


class Gather:
    def __init__(self, run, me, view, rows, cut):
        self.run, self.me, self.view, self.arrived = run, me, view, {}
        self.parts = {1: pl.ds(0, cut), -1: pl.ds(cut, rows - cut)}

    def send(self, hop, way, source=None):
        if hop > 0:
            self.arrived[way, hop - 1].wait_recv()
        block = (self.me.z - way * hop + NZ) % NZ
        there = self.view(block)
        here = there if source is None else source
        if hop == 3:
            here, there = here.at[self.parts[way]], there.at[self.parts[way]]
        self.arrived[way, hop] = self.run.push(here, there, self.me.at_z(way))
        return block

    def end(self):
        for way in (1, -1):
            self.arrived[way, 3].wait_recv()


class Reduce:
    def __init__(self, run, me, own, landed, rows, cut):
        self.run, self.me, self.own, self.landed, self.arrived = run, me, own, landed, {}
        self.parts = {1: pl.ds(0, cut), -1: pl.ds(cut, rows - cut)}

    def send(self, hop, way):
        lane = (1 - way) // 2
        own = self.own((self.me.z + way * (4 - hop) + NZ) % NZ)
        part, rest = self.parts[way], self.parts[-way]
        there = self.landed.at[lane, hop]
        if hop == 0:
            source, there = own.at[part], there.at[part]
        else:
            self.arrived[way, hop - 1].wait_recv()
            source = self.landed.at[lane, hop - 1]
            if hop == 1:
                source[part] = (source[part].astype(F32) + own[part].astype(F32)).astype(BF16)
                source[rest] = own[rest]
            else:
                source[...] = (source[...].astype(F32) + own[...].astype(F32)).astype(BF16)
        self.arrived[way, hop] = self.run.push(source, there, self.me.at_z(way))

    def end(self):
        for way in (1, -1):
            self.arrived[way, 3].wait_recv()
        own = self.own(self.me.z)[...].astype(F32)
        return own + self.landed[0, 3].astype(F32) + self.landed[1, 3].astype(F32)


PUSHES, MOVES = 168, 8
ORDER = (
    "w_other", "w_own", "w_pair_up", "w0", "b_products", "b_over_x",
    "w1", "a_products", "a_first", "a0", "a_rest", "w2",
    "b_own", "b_pass_on_0", "a1", "w3", "b_pass_on_1", "a2",
    "w_over_y", "b_sum_up_0", "b0", "a3", "w_hand_on", "b1",
    "a_over_x", "b_sum_up_1", "b2", "a_end", "w_end", "b3",
    "b_end",
)


def whole_kernel(
    q_ref, g_ref, enc_ref, kw_ref, vw_ref, ids_ref,
    out_q, ids_all, out_enc, out_w,
    q_x, g_x, enc_all, w_all, ids, table, enc_sel, w_t, kv_t, slots_t, scores, grads, score_bf, weight_bf, qg,
    slot_grads, part_a, part_b, w_part, w_pair, w_sum, land_a, land_b, land_w, x_b, b_sum, a_sum, x_a, y_sum, y_land, y_all,
    send_sems, recv_sems, local_sems
):
    me = Place()
    x, z, core = me.x, me.z, me.core
    scale = HEAD_DIM ** (-0.5)
    meet(
        [me.at_x(1), me.at_x(2), me.at_x(3), me.at_z(1), me.at_z(NZ - 1), me.sibling()]
        + [me.at_y(step) for step in range(1, NY)]
        + [me.at_y(step, other=True) for step in range(1, NY)]
    )
    run = Copies(send_sems, recv_sems, local_sems)
    late = []

    in_a, in_b = pl.ds(0, IN_A), pl.ds(IN_A, ENC - IN_A)
    run.move(ids_ref, ids_all.at[x])
    own_enc = run.move(enc_ref, enc_all.at[x, z])
    quarter = quarter_of(me.y)
    own_w = [
        pltpu.make_async_copy(ref.at[quarter], w_all.at[core, quarter, cols(z, TOK)], local_sems.at[MOVES])
        for ref in (kw_ref, vw_ref)
    ]
    for kind in range(2):
        pl.when(core == kind)(own_w[kind].start)
    gather_b = Gather(run, me, lambda block: enc_all.at[x, block, in_b], ENC - IN_A, 64)
    gather_w = Gather(run, me, lambda block: w_all.at[core, quarter, cols(block, TOK)], QUARTER, 64)
    gathers_a = [
        Gather(run, me, lambda block, chunk=chunk: enc_all.at[(x + chunk) % NX, block, in_a], IN_A, 160)
        for chunk in range(NX)
    ]

    def both_ways(gather, hop, source=None):
        for way in (1, -1):
            gather.send(hop, way, source)

    both_ways(gather_b, 0, enc_ref.at[in_b])
    from_x = {}
    for step in (1, 3, 2):
        from_x[NX - step] = run.push(enc_ref.at[in_a], enc_all.at[x, z, in_a], me.at_x(step))
    lists = [run.push(ids_ref, ids_all.at[x], me.at_x(step)) for step in (1, 2, 3)]
    own_w[0].wait()
    both_ways(gather_w, 0)
    both_ways(gathers_a[0], 0, enc_ref.at[in_a])
    inputs_x = {step: [] for step in range(NX)}

    def exchange(src, dst):
        for step in (1, 3, 2):
            copy = run.push(src.at[:, cols((x + step) % NX, WIDTH)], dst.at[x], me.at_x(step))
            inputs_x[NX - step].append(copy)

    exchange(q_ref, q_x)
    own_inputs = [run.move(src.at[:, cols(x, WIDTH)], dst.at[x]) for src, dst in ((q_ref, q_x), (g_ref, g_x))]
    own_enc.wait()
    both_ways(gather_b, 1)
    both_ways(gather_w, 1)
    for chunk in (1, 3):
        from_x[chunk].wait_recv()
        both_ways(gathers_a[chunk], 0)
    both_ways(gather_b, 2)
    both_ways(gather_w, 2)
    from_x[2].wait_recv()
    both_ways(gathers_a[2], 0)
    both_ways(gather_b, 3)
    both_ways(gather_w, 3)
    both_ways(gathers_a[0], 1)
    gather_b.end()
    blocks_b = enc_all.at[x, :, in_b]
    from_x_b = [run.push(blocks_b, blocks_b, me.at_x(step)) for step in (1, 3, 2)]
    exchange(g_ref, g_x)
    gather_w.end()
    own_quarter = w_all.at[core, quarter]
    from_y = [run.push(own_quarter, own_quarter, me.at_y(step)) for step in (1, NY - 1, 2)]
    from_sibling = [run.push(own_quarter, own_quarter, me.sibling())]
    for chunk in (1, 3, 2):
        both_ways(gathers_a[chunk], 1)
    for chunk in (0, 1, 3, 2):
        both_ways(gathers_a[chunk], 2)
    for copy, step in zip(from_y, (3, 1, 2)):
        copy.wait_recv()
        view = w_all.at[core, quarter_of(me.y + step)]
        from_sibling.append(run.push(view, view, me.sibling()))
    for copy in lists:
        copy.wait_recv()
    run.local[0].wait()
    run.move(ids_all, ids).wait()

    def id_of(slot):
        return ids[slot // 4, slot // 2 % 2, slot % 2] & (NX * NZ - 1)

    def first_of(neighbour, after):
        first = SLOTS
        for slot in range(SLOTS - 1, after, -1):
            first = jnp.where(id_of(slot) == neighbour, slot, first)
        return first

    def fill_table(start):
        @pl.loop(start, start + NZ)
        def _(neighbour):
            table[neighbour] = first_of(neighbour, -1)

    fill_table(0)
    for turn, chunk in enumerate((0, 1, 3, 2)):
        both_ways(gathers_a[chunk], 3)
        if turn < 3:
            fill_table((turn + 1) * NZ)
    for slot in range(SLOTS):
        table[NX * NZ + slot] = first_of(id_of(slot), slot)
    for copy in from_sibling:
        copy.wait_recv()
    for kind in range(2):
        for head in range(HEADS_DEV):
            at = kind * WIDTH + head * HEAD_DIM
            w_t[at : at + HEAD_DIM, :] = w_all[kind, :, head * HEAD_DIM : (head + 1) * HEAD_DIM].T
    slot_grads[SLOTS] = jnp.zeros((ENC, NLEN), BF16)
    for chunk in (0, 1, 3, 2):
        gathers_a[chunk].end()
    for copy in from_x_b:
        copy.wait_recv()

    for slot in range(SLOTS):
        neighbour = id_of(slot)
        enc_sel[:, slot * NLEN : (slot + 1) * NLEN] = enc_all[neighbour // NZ, neighbour % NZ]

    @pl.loop(0, 8)
    def _(span):
        here = cols(span, 2 * NLEN)
        chosen = enc_sel[:, here]
        for tile in range(4):
            rows = pl.ds(tile * 512, 512)
            kv_t[rows, here] = dot(w_t[rows, :], chosen).astype(BF16)

    for step in (0, 1, 3, 2):
        source = (x + step) % NX
        if step == 0:
            for copy in own_inputs:
                copy.wait()
        else:
            for copy in inputs_x[step]:
                copy.wait_recv()

        @pl.loop(0, 2)
        def _(turn):
            here, rows = cols(source * 2 + turn, 2 * NLEN), cols(turn, SPAN)
            for head in range(HEADS_DEV):
                lanes, tile = pl.ds(head * HEAD_DIM, HEAD_DIM), pl.ds(head * SPAN, SPAN)
                scores[tile, :] = dot(q_x[source, rows, lanes], kv_t[lanes, here])
                grads[tile, :] = dot(g_x[source, rows, lanes], kv_t[pl.ds(WIDTH + head * HEAD_DIM, HEAD_DIM), here])
            expo = scores[...]
            expo = jnp.exp((expo - jnp.max(expo, axis=-1, keepdims=True)) * scale)
            weights = expo * (1.0 / jnp.sum(expo, axis=-1, keepdims=True))
            weight_bf[...] = weights.astype(BF16)
            weight_grad = grads[...]
            row_delta = jnp.sum(weights * weight_grad, axis=-1, keepdims=True)
            score_bf[...] = (weights * (weight_grad - row_delta) * scale).astype(BF16)
            for head in range(HEADS_DEV):
                lanes, tile = pl.ds(head * HEAD_DIM, HEAD_DIM), pl.ds(head * SPAN, SPAN)
                query, grad = q_x[source, rows, lanes], g_x[source, rows, lanes]
                qg[source, rows, lanes] = dot(score_bf[tile, :], kv_t[lanes, here], 1, 1).astype(BF16)
                slots_t[lanes, here] = dot(query, score_bf[tile, :], 0, 0).astype(BF16)
                slots_t[pl.ds(WIDTH + head * HEAD_DIM, HEAD_DIM), here] = dot(grad, weight_bf[tile, :], 0, 0).astype(BF16)

        if step == 0:
            run.move(qg.at[x], out_q.at[x])
        else:
            late.append(run.push(qg.at[source], out_q.at[x], me.at_x(step)))

    def slot_products(rows):
        @pl.loop(0, 8)
        def _(span):
            here = cols(span, 2 * NLEN)
            both = dot(w_all[0, rows, :], slots_t[0:WIDTH, here]) + dot(w_all[1, rows, :], slots_t[WIDTH:, here])
            both = both.astype(BF16)
            slot_grads[2 * span, rows] = both[:, 0:NLEN]
            slot_grads[2 * span + 1, rows] = both[:, NLEN:]

        for slot in range(SLOTS - 2, -1, -1):
            slot_grads[slot, rows] = slot_grads[slot, rows] + slot_grads[table[NX * NZ + slot], rows]

    def neighbour_a(at_x, at_z):
        part_a[at_x, at_z] = slot_grads[table[at_x * NZ + at_z], out_a]

    def sum_b(at_x):
        @pl.loop(0, NZ)
        def _(order):
            part_b[at_x, order] = slot_grads[table[at_x * NZ + (z + 3 + order) % NZ], out_b]

    out_a, out_b = pl.ds(0, OUT_A), pl.ds(OUT_A, ENC - OUT_A)
    half = (ENC - OUT_A) // 2
    low, high = pl.ds(0, half), pl.ds(half, half)
    far, right, left = (x + 2) % NX, (x + 1) % NX, (x + 3) % NX
    groups, bounds = [pl.ds(0, 3), pl.ds(3, 5)], [(0, 3), (3, 8)]
    y = me.y
    going = {}
    reduces_a = [
        Reduce(run, me, lambda block, chunk=chunk: part_a.at[chunk, block], land_a.at[chunk], OUT_A, OUT_A // 2)
        for chunk in range(NX)
    ]
    reduce_b = Reduce(run, me, lambda block: b_sum.at[(block - z - 3 + 2 * NZ) % NZ], land_b, ENC - OUT_A, half)
    reduce_w = Reduce(run, me, lambda block: w_sum.at[block], land_w, ENC, ENC // 2)

    def turn(reduces, hop):
        for reduce in reduces:
            for way in (1, -1):
                reduce.send(hop, way)

    def a_first():
        @pl.loop(0, NX)
        def _(at_x):
            neighbour_a(at_x, (z + 4) % NZ)

    def a_rest():
        @pl.loop(0, NX * (NZ - 1))
        def _(index):
            neighbour_a(index % NX, (z + 5 + index // NX) % NZ)

    def a_over_x():
        for chunk in range(NX):
            a_sum[chunk] = reduces_a[chunk].end().astype(BF16)
        going["a"] = [run.push(a_sum.at[(x + step) % NX], x_a.at[step - 1], me.at_x(step)) for step in (1, 2, 3)]

    def a_end():
        total = a_sum[x].astype(F32)
        for step in range(NX - 1):
            going["a"][step].wait_recv()
            total += x_a[step].astype(F32)
        out_enc[out_a] = total.astype(BF16)

    def b_over_x():
        for at_x in (far, right, left):
            sum_b(at_x)
        going["b"] = []
        for group in groups:
            via_left = run.push(part_b.at[far, group, low], x_b.at[0, group], me.at_x(1))
            via_right = run.push(part_b.at[far, group, high], x_b.at[1, group], me.at_x(3))
            high_left = run.push(part_b.at[right, group, high], x_b.at[2, group], me.at_x(1))
            low_right = run.push(part_b.at[left, group, low], x_b.at[3, group], me.at_x(3))
            going["b"].append([via_left, via_right, high_left, low_right])

    def add_on(target, landed, rows, blocks):
        @pl.loop(*blocks)
        def _(block):
            landed[block] = (landed[block].astype(F32) + part_b[target, block, rows].astype(F32)).astype(BF16)

    def b_pass_on(at):
        group, copies = groups[at], going["b"][at]
        copies[0].wait_recv()
        add_on(right, x_b.at[0], low, bounds[at])
        copies[0] = run.push(x_b.at[0, group], x_b.at[4, group], me.at_x(1))
        copies[1].wait_recv()
        add_on(left, x_b.at[1], high, bounds[at])
        copies[1] = run.push(x_b.at[1, group], x_b.at[5, group], me.at_x(3))

    def b_sum_up(at):
        for copy in going["b"][at]:
            copy.wait_recv()

        @pl.loop(*bounds[at])
        def _(block):
            for rows, first, second in ((low, 3, 4), (high, 2, 5)):
                total = part_b[x, block, rows].astype(F32) + x_b[first, block].astype(F32)
                b_sum[block, rows] = (total + x_b[second, block].astype(F32)).astype(BF16)

    def b_end():
        out_enc[out_b] = reduce_b.end().astype(BF16)

    def weight_products(kind):
        @pl.loop(0, 4)
        def _(tile):
            rows = pl.ds(pl.multiple_of(kind * WIDTH + tile * 256, 256), 256)
            product = dot(enc_sel[...], slots_t[rows, :], 1, 1).astype(BF16)
            w_part[kind, 2 * tile] = product[:, 0:TOK]
            w_part[kind, 2 * tile + 1] = product[:, TOK:]

    def w_other():
        weight_products(1 - core)
        going["pair"] = run.push(w_part.at[1 - core], w_pair, me.sibling())

    def w_pair_up():
        going["pair"].wait_recv()

        @pl.loop(0, NZ)
        def _(block):
            w_sum[block] = (w_part[core, block].astype(F32) + w_pair[block].astype(F32)).astype(BF16)

    def w_over_y():
        y_sum[pl.ds(0, ENC)] = reduce_w.end().astype(BF16)
        y_sum[pl.ds(ENC, 64)] = jnp.zeros((64, TOK), BF16)
        going["y"] = [
            run.push(y_sum.at[rows_of((y + step) % NY)], y_land.at[step - 1], me.at_y(step)) for step in range(1, NY)
        ]

    def w_hand_on():
        total = y_sum[rows_of(y)].astype(F32)
        for step in range(NY - 1):
            going["y"][step].wait_recv()
            total += y_land[step].astype(F32)
        y_all[core, rows_of(y)] = total.astype(BF16)
        own_rows = y_all.at[core, rows_of(y)]
        going["y"] = [run.push(own_rows, own_rows, me.at_y(step)) for step in range(1, NY)]
        going["y"] += [run.push(own_rows, own_rows, me.at_y(step, other=True)) for step in range(NY)]

    def w_end():
        for copy in going["y"]:
            copy.wait_recv()
        for kind in range(2):
            out_w[kind] = y_all[kind, pl.ds(0, ENC)].astype(F32)

    steps = {
        "a_products": lambda: slot_products(out_a),
        "a_first": a_first,
        "a_rest": a_rest,
        "a0": lambda: turn(reduces_a, 0),
        "a1": lambda: turn(reduces_a, 1),
        "a2": lambda: turn(reduces_a, 2),
        "a3": lambda: turn(reduces_a, 3),
        "a_over_x": a_over_x,
        "a_end": a_end,
        "b_products": lambda: slot_products(out_b),
        "b_over_x": b_over_x,
        "b_own": lambda: sum_b(x),
        "b_pass_on_0": lambda: b_pass_on(0),
        "b_pass_on_1": lambda: b_pass_on(1),
        "b_sum_up_0": lambda: b_sum_up(0),
        "b_sum_up_1": lambda: b_sum_up(1),
        "b0": lambda: turn([reduce_b], 0),
        "b1": lambda: turn([reduce_b], 1),
        "b2": lambda: turn([reduce_b], 2),
        "b3": lambda: turn([reduce_b], 3),
        "b_end": b_end,
        "w_other": w_other,
        "w_own": lambda: weight_products(core),
        "w_pair_up": w_pair_up,
        "w0": lambda: turn([reduce_w], 0),
        "w1": lambda: turn([reduce_w], 1),
        "w2": lambda: turn([reduce_w], 2),
        "w3": lambda: turn([reduce_w], 3),
        "w_over_y": w_over_y,
        "w_hand_on": w_hand_on,
        "w_end": w_end,
    }
    for name in ORDER:
        steps[name]()

    for copy in late:
        copy.wait_recv()
    for copy in run.remote:
        copy.wait_send()
    run.local[-1].wait()


def quarter_of(index):
    return pl.ds(pl.multiple_of(index % 4 * QUARTER, QUARTER), QUARTER)


def rows_of(index):
    return pl.ds(pl.multiple_of(index * 64, 64), 64)


def whole(queries, out_grad, enc_t, key_weight, value_weight, ids):
    anywhere, vmem = pl.BlockSpec(memory_space=pl.ANY), pl.BlockSpec(memory_space=pltpu.VMEM)
    enc_b = ENC - OUT_A
    bf = lambda *shape: pltpu.VMEM(shape, BF16)
    f32 = lambda *shape: pltpu.VMEM(shape, F32)
    return pl.pallas_call(
        whole_kernel,
        out_shape=[
            jax.ShapeDtypeStruct((NX, TOK, WIDTH), BF16),
            jax.ShapeDtypeStruct((NX, 2, 2), jnp.int32),
            jax.ShapeDtypeStruct((ENC, NLEN), BF16),
            jax.ShapeDtypeStruct((2, ENC, TOK), F32),
        ],
        in_specs=[anywhere] * 6,
        out_specs=[anywhere, anywhere, vmem, vmem],
        scratch_shapes=[
            bf(NX, TOK, WIDTH),
            bf(NX, TOK, WIDTH),
            bf(NX, NZ, ENC, NLEN),
            bf(2, ENC, WIDTH),
            pltpu.SMEM((NX, 2, 2), jnp.int32),
            pltpu.SMEM((NX * NZ + SLOTS,), jnp.int32),
            bf(ENC, SLOTS * NLEN),
            bf(2 * WIDTH, ENC),
            bf(2 * WIDTH, SLOTS * NLEN),
            bf(2 * WIDTH, SLOTS * NLEN),
            f32(HEADS_DEV * SPAN, 2 * NLEN),
            f32(HEADS_DEV * SPAN, 2 * NLEN),
            bf(HEADS_DEV * SPAN, 2 * NLEN),
            bf(HEADS_DEV * SPAN, 2 * NLEN),
            bf(NX, TOK, WIDTH),
            bf(SLOTS + 1, ENC, NLEN),
            bf(NX, NZ, OUT_A, NLEN),
            bf(NX, NZ, enc_b, NLEN),
            bf(2, NZ, ENC, TOK),
            bf(NZ, ENC, TOK),
            bf(NZ, ENC, TOK),
            bf(NX, 2, 4, OUT_A, NLEN),
            bf(2, 4, enc_b, NLEN),
            bf(2, 4, ENC, TOK),
            bf(6, NZ, enc_b // 2, NLEN),
            bf(NZ, enc_b, NLEN),
            bf(NX, OUT_A, NLEN),
            bf(NX - 1, OUT_A, NLEN),
            bf(512, TOK),
            bf(NY - 1, 64, TOK),
            bf(2, 512, TOK),
            pltpu.SemaphoreType.DMA((PUSHES,)),
            pltpu.SemaphoreType.DMA((PUSHES,)),
            pltpu.SemaphoreType.DMA((MOVES + 1,)),
        ],
        compiler_params=pltpu.CompilerParams(collective_id=0, has_side_effects=True, vmem_limit_bytes=VMEM_LIMIT),
    )(queries, out_grad, enc_t, key_weight, value_weight, ids)


def close_kernel(q_ref, enc_ref, w_ref, out_q, out_enc, out_k, out_v, sems):
    copies = [
        pltpu.make_async_copy(q_ref.at[source], out_q.at[:, pl.ds(source * WIDTH, WIDTH)], sems.at[source])
        for source in range(NX)
    ]
    copies.append(pltpu.make_async_copy(enc_ref, out_enc, sems.at[4]))
    copies.append(pltpu.make_async_copy(w_ref.at[0], out_k, sems.at[5]))
    copies.append(pltpu.make_async_copy(w_ref.at[1], out_v, sems.at[6]))
    for copy in copies:
        copy.start()
    for copy in copies:
        copy.wait()


def close(query_grads, enc_grad, weight_grads):
    anywhere, vmem = pl.BlockSpec(memory_space=pl.ANY), pl.BlockSpec(memory_space=pltpu.VMEM)
    return pl.pallas_call(
        close_kernel,
        out_shape=[
            jax.ShapeDtypeStruct((TOK, NX * WIDTH), BF16),
            jax.ShapeDtypeStruct((ENC, NLEN), BF16),
            jax.ShapeDtypeStruct((ENC, TOK), F32),
            jax.ShapeDtypeStruct((ENC, TOK), F32),
        ],
        in_specs=[anywhere] * 3,
        out_specs=[vmem] * 4,
        scratch_shapes=[pltpu.SemaphoreType.DMA((7,))],
        compiler_params=pltpu.CompilerParams(vmem_limit_bytes=VMEM_LIMIT),
    )(query_grads, enc_grad, weight_grads)


def local(queries, out_grad, encodings, key_weight, value_weight, nbr_ids):
    enc_t = jnp.swapaxes(encodings[0], 0, 1)
    query_grads, _, enc_grad, weight_grads = whole(queries, out_grad, enc_t, key_weight, value_weight, nbr_ids)
    query_grad, enc_grad, key_grad, value_grad = close(query_grads, enc_grad, weight_grads)
    return query_grad, jnp.swapaxes(enc_grad, 0, 1)[None], key_grad, value_grad


def solution(mesh):
    in_specs = (
        P(("dp", "group"), None),
        P(("dp", "group"), None),
        P(("dp", "group"), None, None),
        P(None, "group"),
        P(None, "group"),
        P(("dp", "group"), None),
    )
    out_specs = (
        P(("dp", "group"), None),
        P(("dp", "group"), None, None),
        P(None, "group"),
        P(None, "group"),
    )
    return jax.shard_map(local, mesh=mesh, in_specs=in_specs, out_specs=out_specs, check_vma=False)
```
